128 devices in a mesh: group: 2 (over core), wide: 64 (over y, z, x).
Axes of the slice: x: 4, y: 4, z: 4, core: 2. Of those that a mesh axis runs over, the one named last changes fastest.
Arguments:
- hot_table: bfloat16 [4096, 256], replicated, may hold values from -6 to 6
- tail_table: bfloat16 [524288, 256], P('wide'), may hold values from -6 to 6
- word_table: bfloat16 [4096, 256], replicated, may hold values from -6 to 6
- out_table: bfloat16 [8192, 256], replicated, may hold values from -1.796875 to 1.796875
- w_first: bfloat16 [600, 1024], replicated, may hold values from -0.5 to 0.5
- b_first: bfloat16 [1024], replicated, may hold values from -1.5 to 1.5
- w_second: bfloat16 [1024, 512], replicated, may hold values from -0.25 to 0.25
- b_second: bfloat16 [512], replicated, may hold values from -1.5 to 1.5
- w_third: bfloat16 [512, 256], replicated, may hold values from -0.5 to 0.5
- b_third: bfloat16 [256], replicated, may hold values from -1.5 to 1.5
- dense_feats: bfloat16 [131072, 88], P(('group', 'wide')), may hold values from -6 to 6
- hist_ids: int32 [131072, 50], P(('group', 'wide')), may hold values from 0 to 12287, as said below
- hist_len: int32 [131072], P(('group', 'wide')), may hold values from 1 to 50
- search_ids: int32 [131072, 50], P(('group', 'wide')), may hold values from 0 to 4095
- search_len: int32 [131072], P(('group', 'wide')), may hold values from 1 to 50
- requests: int32 [8192, 128], P(('group', 'wide')), may hold values from -1 to 8191, as said below
- labels: int32 [131072], P(('group', 'wide')), may hold values from 0 to 8191
- negatives: int32 [5000], replicated, may hold values from 0 to 8191, as said below
Outputs:
- loss_value: float32 [], replicated
- hot_grad: float32 [4096, 256], replicated
- tail_grad: float32 [524288, 256], P('wide')
- word_grad: float32 [4096, 256], replicated
- out_grad: float32 [8192, 256], replicated
- w_first_grad: float32 [600, 1024], replicated
- b_first_grad: float32 [1024], replicated
- w_second_grad: float32 [1024, 512], replicated
- b_second_grad: float32 [512], replicated
- w_third_grad: float32 [512, 256], replicated
- b_third_grad: float32 [256], replicated
The draws below stay inside these ranges and needn't reach their ends.
Inputs may be any that keep to these rules, and one draw needn't show every extreme that they name: `requests`: row p * 64 + o belongs to device p and owner o: its first entries name rows of that owner's 8192 rows, the rest are -1; at least 64 are filled and in every draw some blocks are full. `hist_ids`: an entry below 4096 names a row of hot_table; an entry v of 4096 or more names the device's request slot v - 4096 (owner (v - 4096) // 128), which is always a filled slot. `negatives`: all different.
All inputs are finite; a program needn't handle non-finite values.
Results may differ from the reference program's by a relative error of at most 0.012.
The reference program's roundings to bfloat16 on the way count: a program that leaves them out, or rounds other values in their place, can miss the bound.
Values may be sent and summed in bfloat16 or wider, within the bound.
No kernel may reach another device: no remote copies, remote signals or barrier semaphores. Data moves between devices by JAX's collectives and lax.ppermute only.
A program may use at most 256 MiB of HBM per device.

```python
import math
import jax
import jax.numpy as jnp
import numpy as np
from jax import lax

D = 256
H1 = 1024
H2 = 512
DENSE = 88
HLEN = 50
SLEN = 50
NEG = 5000
HOT = 4096
WORDS = 4096
OUTROWS = 8192
TAIL_DEV = 8192
CAP = 128
EX_DEV = 1024
IN = 600
EXAMPLES = 131072
TAIL_ROWS = 524288
N_GROUP = 2
N_WIDE = 64


def block_counts(key):
    count_key = jax.random.fold_in(key, 11)
    devices = N_GROUP * N_WIDE
    counts = jax.random.randint(count_key, (devices, N_WIDE), CAP // 2, CAP + 1)
    owner_of = jnp.arange(N_WIDE)[None, :]
    device_of = jnp.arange(devices)[:, None]
    return jnp.where(owner_of == device_of % N_WIDE, CAP, counts)


def draw_requests(key, part):
    counts = block_counts(key)
    key = jax.random.fold_in(key, 3)
    devices = N_GROUP * N_WIDE
    row_ids = jax.random.randint(key, (devices, N_WIDE, CAP), 0, TAIL_DEV)
    filled = jnp.arange(CAP)[None, None, :] < counts[:, :, None]
    return jnp.where(filled, row_ids, -1).reshape(devices * N_WIDE, CAP).astype(jnp.int32)


def draw_hist_ids(key, part):
    counts = block_counts(key)
    key = jax.random.fold_in(key, 5)
    first, second, third, fourth = jax.random.split(key, 4)
    examples = EX_DEV * N_GROUP * N_WIDE
    shape = (examples, HLEN)
    choose_hot = jax.random.randint(first, shape, 0, 2) == 0
    hot_ids = jax.random.randint(second, shape, 0, HOT)
    owner_ids = jax.random.randint(third, shape, 0, N_WIDE)
    device_ids = (jnp.arange(examples) // EX_DEV)[:, None]
    limits = counts[device_ids, owner_ids]
    slot_ids = jax.random.randint(fourth, shape, 0, limits)
    tail_ids = HOT + owner_ids * CAP + slot_ids
    return jnp.where(choose_hot, hot_ids, tail_ids).astype(jnp.int32)


def draw_negatives(key, part):
    key = jax.random.fold_in(key, 7)
    return jax.random.permutation(key, OUTROWS)[:NEG].astype(jnp.int32)


def set_ends(values, stream_key, low, top_value):
    shape = values.shape
    place = [jax.random.randint(jax.random.fold_in(stream_key, axis), (), 0, shape[axis]) for axis in range(len(shape))]
    values = values.at[tuple(place)].set(low)
    longest = shape.index(max(shape))
    place[longest] = (place[longest] + 1) % shape[longest]
    return values.at[tuple(place)].set(top_value)


def level_of(own_key, dims, cuts, low, high):
    level, own = 1.0, jax.random.fold_in(own_key, 6)
    for position, shards_of in cuts:
        heights = jnp.exp(jax.random.uniform(jax.random.fold_in(own, position), (shards_of,), jnp.float32, low / len(cuts), high / len(cuts)))
        level = level * jnp.repeat(heights, dims[position] // shards_of).reshape([-1 if axis == position else 1 for axis in range(len(dims))])
    return level


def cumulative_ranks(amount, skew):
    portions = [(1 << 20) // math.isqrt(grade ** skew) + 1 for grade in range(1, amount + 1)]
    spread = 1 + sum(portions) // (1 << 30)
    return np.cumsum(np.array([max(1, weight // spread) for weight in portions]))


def skewed_ids(key, extent, amount, slope):
    table = cumulative_ranks(amount, slope)
    ticket = jax.random.randint(jax.random.fold_in(key, 1), extent, 0, int(table[amount - 1]))
    standing = jnp.searchsorted(jnp.asarray(table, jnp.int32), ticket, side="right")
    return jax.random.permutation(jax.random.fold_in(key, 2), amount)[standing].astype(jnp.int32)


def noise(key, extent, spread, limit, cuts=(), held_as=jnp.bfloat16):
    result = jax.random.normal(key, extent, jnp.float32) * spread
    if len(cuts) > 0:
        result = level_of(key, extent, cuts, -0.22, 0.18) * result
    return jnp.clip(result, min=-limit, max=limit).astype(held_as)


def setup_inputs(seed: int = 0) -> dict:
    splits = jax.random.split(jax.random.key(seed), 19)
    hot_table = noise(splits[0], (HOT, D), 1.0, 6.0)
    tail_table = noise(splits[1], (TAIL_ROWS, D), 1.0, 6.0, ((0, 64),))
    word_table = noise(splits[2], (WORDS, D), 1.0, 6.0)
    out_table = noise(splits[3], (OUTROWS, D), 0.3, 1.796875)
    w_first = noise(splits[4], (IN, H1), (IN // 4) ** -0.5, 0.5)
    b_first = noise(splits[5], (H1,), 0.3, 1.5)
    w_second = noise(splits[6], (H1, H2), (H1 // 2) ** -0.5, 0.25)
    b_second = noise(splits[7], (H2,), 0.3, 1.5)
    w_third = noise(splits[8], (H2, D), (H2 // 4) ** -0.5, 0.5)
    b_third = noise(splits[9], (D,), 0.3, 1.5)
    dense_feats = noise(splits[10], (EXAMPLES, DENSE), 1.0, 6.0, ((0, 128),))
    hist_ids = draw_hist_ids(jax.random.fold_in(splits[18], 71), 0)
    hist_len = set_ends(jax.random.randint(splits[12], (EXAMPLES,), 1, HLEN + 1), jax.random.fold_in(splits[12], 1), 1, HLEN).astype(jnp.int32)
    search_ids = set_ends(skewed_ids(splits[13], (EXAMPLES, SLEN), WORDS, 2), jax.random.fold_in(splits[13], 3), 0, WORDS - 1).astype(jnp.int32)
    search_len = set_ends(jax.random.randint(splits[14], (EXAMPLES,), 1, SLEN + 1), jax.random.fold_in(splits[14], 1), 1, SLEN).astype(jnp.int32)
    requests = draw_requests(jax.random.fold_in(splits[18], 71), 0)
    labels = set_ends(jax.random.randint(splits[16], (EXAMPLES,), 0, OUTROWS), jax.random.fold_in(splits[16], 1), 0, OUTROWS - 1).astype(jnp.int32)
    negatives = draw_negatives(jax.random.fold_in(splits[18], 71), 0)
    return {"hot_table": hot_table, "tail_table": tail_table, "word_table": word_table, "out_table": out_table, "w_first": w_first, "b_first": b_first, "w_second": w_second, "b_second": b_second, "w_third": w_third, "b_third": b_third, "dense_feats": dense_feats, "hist_ids": hist_ids, "hist_len": hist_len, "search_ids": search_ids, "search_len": search_len, "requests": requests, "labels": labels, "negatives": negatives}


@jax.custom_vjp
def low(v):
    return lax.optimization_barrier(v.astype(jnp.bfloat16)).astype(jnp.float32)

@jax.custom_vjp
def low_back(v):
    return v

def low_keep(v):
    return (low(v), None)

def low_pass(kept, grad):
    return (grad,)

def back_keep(v):
    return (v, None)

def back_low(kept, grad):
    return (low(grad),)
low.defvjp(low_keep, low_pass)
low_back.defvjp(back_keep, back_low)

def matmul(first_op, second_op):
    return jnp.dot(first_op, second_op, precision=lax.Precision.HIGHEST)

def pooled(table, id_table, lengths):
    picked = table[id_table]
    in_range = (jnp.arange(id_table.shape[1])[None, :] < lengths[:, None]).astype(jnp.float32)
    return lax.optimization_barrier(jnp.sum(picked * in_range[:, :, None], axis=1)) / lengths[:, None].astype(jnp.float32)

def forward(hot_table, fetched, word_table, out_table, w_first, b_first, w_second, b_second, w_third, b_third, dense_feats, hist_ids, hist_len, search_ids, search_len, labels, negatives):
    source = jnp.concatenate([hot_table, fetched], axis=0)
    hist_mean = pooled(source, hist_ids, hist_len)
    search_mean = pooled(word_table, search_ids, search_len)
    inputs = low(jnp.concatenate([hist_mean, search_mean, dense_feats], axis=1))
    act_first = low(jax.nn.gelu(low_back(matmul(inputs, w_first) + b_first)))
    act_second = low(jax.nn.gelu(low_back(matmul(act_first, w_second) + b_second)))
    user = low(low_back(matmul(act_second, w_third) + b_third))
    neg_logits = matmul(user, out_table[negatives].T)
    pos_logits = lax.optimization_barrier(jnp.sum(user * out_table[labels], axis=1))
    logits = low_back(jnp.concatenate([pos_logits[:, None], neg_logits], axis=1))
    per_example = jax.nn.logsumexp(logits, axis=1) - logits[:, 0]
    return (jnp.sum(per_example) / EX_DEV, jnp.sum(per_example))

def reference(hot_table, tail_table, word_table, out_table, w_first, b_first, w_second, b_second, w_third, b_third, dense_feats, hist_ids, hist_len, search_ids, search_len, requests, labels, negatives):
    weights = [x.astype(jnp.float32) for x in (hot_table, word_table, out_table, w_first, b_first, w_second, b_second, w_third, b_third)]
    tail_float = tail_table.astype(jnp.float32)
    dense_float = dense_feats.astype(jnp.float32)
    owner_base = (jnp.arange(N_WIDE * CAP) // CAP * TAIL_DEV).astype(jnp.int32)
    device_count = N_GROUP * N_WIDE

    def device_block(totals, device):
        start = (device * EX_DEV).astype(jnp.int32)

        def cut(array):
            return lax.dynamic_slice_in_dim(array, start, EX_DEV, 0)
        asked_ids = lax.dynamic_slice_in_dim(requests, (device * N_WIDE).astype(jnp.int32), N_WIDE, 0).reshape(-1)
        filled = asked_ids >= 0
        global_rows = (owner_base + jnp.clip(asked_ids, 0, TAIL_DEV - 1)).astype(jnp.int32)
        fetched = jnp.where(filled[:, None], tail_float[global_rows], jnp.float32(0.0))
        hot_f, word_f, out_f, w1_f, b1_f, w2_f, b2_f, w3_f, b3_f = weights

        def objective(hot_v, fetched_v, word_v, out_v, w1_v, b1_v, w2_v, b2_v, w3_v, b3_v):
            return forward(hot_v, fetched_v, word_v, out_v, w1_v, b1_v, w2_v, b2_v, w3_v, b3_v, cut(dense_float), cut(hist_ids), cut(hist_len), cut(search_ids), cut(search_len), cut(labels), negatives)
        value, pull, loss_sum = jax.vjp(objective, hot_f, fetched, word_f, out_f, w1_f, b1_f, w2_f, b2_f, w3_f, b3_f, has_aux=True)
        gradients = pull(jnp.float32(1.0))
        tail_total = totals[1].at[global_rows].add(jnp.where(filled[:, None], gradients[1], jnp.float32(0.0)))
        dense_totals = tuple((t + g for t, g in zip(totals[0], gradients[:1] + gradients[2:])))
        return ((dense_totals, tail_total, totals[2] + loss_sum), None)
    initial = (tuple((jnp.zeros(w.shape, jnp.float32) for w in weights)), jnp.zeros(tail_float.shape, jnp.float32), jnp.float32(0.0))
    totals, unused = lax.scan(device_block, initial, jnp.arange(device_count))
    dense_totals, tail_total, loss_sum = totals
    hot_g, word_g, out_g, w1_g, b1_g, w2_g, b2_g, w3_g, b3_g = dense_totals
    return (loss_sum / (EX_DEV * device_count), hot_g, tail_total, word_g, out_g, w1_g, b1_g, w2_g, b2_g, w3_g, b3_g)
```

```python
import functools

import jax
import jax.numpy as jnp
from jax import lax
from jax.experimental import pallas as pl
from jax.experimental.pallas import tpu as pltpu
from jax.sharding import PartitionSpec as P

BF = jnp.bfloat16
F32 = jnp.float32
LANES = 128
MIB = 1024 * 1024


def params(mib):
    return pltpu.CompilerParams(vmem_limit_bytes=mib * MIB)


def whole_vmem():
    return pl.BlockSpec(memory_space=pltpu.VMEM)


def whole_smem():
    return pl.BlockSpec(memory_space=pltpu.SMEM)


def counts_body(cuts, ids_ref, hot_ref, word_ref, *refs):
    count_refs = refs[: len(cuts)]
    hist_ref, word_sum_ref, scratch, low_ref, high_ref = refs[len(cuts) :]
    block = ids_ref.shape[0]
    groups = sum(cuts)
    rows = groups + 8
    ids = ids_ref[...]
    low_ref[...] = (ids & (LANES - 1)).astype(F32)
    place = lax.broadcasted_iota(jnp.int32, ids.shape, 0) & 7
    high_ref[...] = (jnp.where(ids < 0, -64, ids >> 7) + place).astype(F32)
    low_iota = lax.broadcasted_iota(jnp.int32, (LANES, LANES), 0).astype(BF)
    high_iota = lax.broadcasted_iota(jnp.int32, (rows, LANES), 0).astype(BF)
    one = jnp.ones((), BF)
    zero = jnp.zeros((), BF)
    unroll = block

    def build(i, carry):
        for k in range(unroll):
            e = i * unroll + k
            low = jnp.broadcast_to(low_ref[pl.ds(e, 1), :], (LANES, LANES)).astype(BF)
            high = jnp.broadcast_to(high_ref[pl.ds(e, 1), :], (rows, LANES)).astype(BF)
            low_hot = jnp.where(low_iota == low, one, zero)
            high_hot = jnp.where(high_iota == high, one, zero)
            scratch[pl.ds(pl.multiple_of(e * rows, 8), rows), :] = right_product(high_hot, low_hot)
        return carry

    lax.fori_loop(0, block // unroll, build, 0)

    def regroup(i, carry):
        base = i * 16 * rows
        here = pl.ds(pl.multiple_of(i * 16, 16), 16)
        g = 0
        for ref, cut in zip(count_refs, cuts):
            for c in range(cut):
                upper = scratch[pl.ds(base + g, 8, stride=rows + 1), :]
                lower = scratch[pl.ds(base + 8 * rows + g, 8, stride=rows + 1), :]
                both = jnp.concatenate([upper, lower], axis=0)
                ref[here, c * LANES : (c + 1) * LANES] = both.astype(BF)
                g += 1
        return carry

    lax.fori_loop(0, block // 16, regroup, 0)
    hist_ref[...] = jnp.dot(count_refs[0][...], hot_ref[...], preferred_element_type=F32)
    word_sum_ref[...] = jnp.dot(count_refs[-1][...], word_ref[...], preferred_element_type=F32)


def counts_call(ids, hot, word, tail_rows, block=128):
    n = ids.shape[0]
    feat = hot.shape[1]
    widths = (hot.shape[0], tail_rows, word.shape[0])
    cuts = tuple(w // LANES for w in widths)
    rows_of = lambda w: pl.BlockSpec((block, w), lambda i: (i, 0))
    fixed = lambda s: pl.BlockSpec(s, lambda i: (0, 0))
    return pl.pallas_call(
        functools.partial(counts_body, cuts),
        grid=(n // block,),
        in_specs=[rows_of(LANES), fixed(hot.shape), fixed(word.shape)],
        out_specs=[rows_of(w) for w in widths] + [rows_of(feat)] * 2,
        out_shape=[jax.ShapeDtypeStruct((n, w), BF) for w in widths]
        + [jax.ShapeDtypeStruct((n, feat), F32)] * 2,
        scratch_shapes=[pltpu.VMEM((block * (sum(cuts) + 8), LANES), F32)]
        + [pltpu.VMEM((block, LANES), F32)] * 2,
        compiler_params=params(56),
        name="counts",
    )(ids, hot, word)


def gather_body(unroll, ids_ref, table_ref, out_ref, wide, picked):
    rows = table_ref.shape[0]
    count = out_ref.shape[0]

    def widen(i, carry):
        t = table_ref[pl.ds(pl.multiple_of(i * 64, 64), 64), :].astype(F32)
        wide[pl.ds(i * 128, 64, stride=2), :] = t[:, :LANES]
        wide[pl.ds(i * 128 + 1, 64, stride=2), :] = t[:, LANES:]
        return carry

    lax.fori_loop(0, rows // 64, widen, 0)

    def pick(i, carry):
        for k in range(unroll):
            at = i * unroll + k
            picked[pl.ds(at * 2, 2), :] = wide[pl.ds(ids_ref[at] * 2, 2), :]
        return carry

    lax.fori_loop(0, count // unroll, pick, 0)

    def join(i, carry):
        left = picked[pl.ds(i * 128, 64, stride=2), :]
        right = picked[pl.ds(i * 128 + 1, 64, stride=2), :]
        out_ref[pl.ds(pl.multiple_of(i * 64, 64), 64), :] = jnp.concatenate(
            [left, right], axis=1
        ).astype(BF)
        return carry

    lax.fori_loop(0, count // 64, join, 0)


def gather_call(ids, table, unroll=32):
    rows, feat = table.shape
    count = ids.shape[0]
    return pl.pallas_call(
        functools.partial(gather_body, unroll),
        in_specs=[whole_smem(), whole_vmem()],
        out_specs=whole_vmem(),
        out_shape=jax.ShapeDtypeStruct((count, feat), BF),
        scratch_shapes=[
            pltpu.VMEM((2 * rows, LANES), F32),
            pltpu.VMEM((2 * count, LANES), F32),
        ],
        compiler_params=params(48),
        name="gather_rows",
    )(ids, table)


def add_rows_body(unroll, ids_ref, again_ref, clash_ref, rows_ref, out_ref, total_a, total_b, wide):
    count = rows_ref.shape[0]
    rows = out_ref.shape[0]

    def clear(i, carry):
        for total in (total_a, total_b):
            total[pl.ds(pl.multiple_of(i * 256, 256), 256), :] = jnp.zeros((256, LANES), F32)
        return carry

    lax.fori_loop(0, rows // 128, clear, 0)

    def widen(i, carry):
        t = rows_ref[pl.ds(pl.multiple_of(i * 128, 128), 128), :].astype(F32)
        wide[pl.ds(i * 256, 128, stride=2), :] = t[:, :LANES]
        wide[pl.ds(i * 256 + 1, 128, stride=2), :] = t[:, LANES:]
        return carry

    lax.fori_loop(0, count // 128, widen, 0)

    def given(at):
        return wide[pl.ds(at * 2, 2), :]

    def add(i, carry):
        for total, base in ((total_a, i * 2 * unroll), (total_b, (i * 2 + 1) * unroll)):
            places = [pl.ds(ids_ref[base + k] * 2, 2) for k in range(unroll)]
            sums = [total[p, :] + given(base + k) for k, p in enumerate(places)]
            for p, v in zip(places, sums):
                total[p, :] = v
        return carry

    lax.fori_loop(0, count // (2 * unroll), add, 0)

    groups = count // unroll
    section = 16

    def check(i, carry):
        @pl.when(clash_ref[groups + i] != 0)
        def _():
            def add_again(j, inner):
                group = i * section + j

                @pl.when(clash_ref[group] != 0)
                def _():
                    for k in range(unroll):
                        p = pl.ds(again_ref[group * unroll + k] * 2, 2)
                        total_a[p, :] = total_a[p, :] + given(group * unroll + k)

                return inner

            lax.fori_loop(0, section, add_again, 0)

        return carry

    lax.fori_loop(0, groups // section, check, 0)

    def join(i, carry):
        left = pl.ds(i * 256, 128, stride=2)
        right = pl.ds(i * 256 + 1, 128, stride=2)
        both = [total_a[p, :] + total_b[p, :] for p in (left, right)]
        out_ref[pl.ds(pl.multiple_of(i * 128, 128), 128), :] = jnp.concatenate(both, axis=1).astype(
            out_ref.dtype
        )
        return carry

    lax.fori_loop(0, rows // 128, join, 0)


def row_plan(ids, rows, unroll):
    grouped = ids.reshape(-1, unroll)
    spare = rows + lax.broadcasted_iota(jnp.int32, grouped.shape, 1)
    earlier = lax.broadcasted_iota(jnp.int32, (unroll, unroll), 1) < lax.broadcasted_iota(
        jnp.int32, (unroll, unroll), 0
    )
    same = (grouped[:, :, None] == grouped[:, None, :]) & earlier[None]
    twice = jnp.any(same, axis=2) & (grouped >= 0)
    once = jnp.where((grouped >= 0) & ~twice, grouped, spare)
    again = jnp.where(twice, grouped, spare)
    clash = jnp.any(twice, axis=1).astype(jnp.int32)
    sections = jnp.max(clash.reshape(-1, 16), axis=1)
    return once.reshape(-1), again.reshape(-1), jnp.concatenate([clash, sections])


def add_rows_call(plan, given, rows, unroll):
    count, feat = given.shape
    return pl.pallas_call(
        functools.partial(add_rows_body, unroll),
        in_specs=[whole_smem()] * 3 + [whole_vmem()],
        out_specs=whole_vmem(),
        out_shape=jax.ShapeDtypeStruct((rows, feat), BF),
        scratch_shapes=[pltpu.VMEM((2 * (rows + unroll), LANES), F32)] * 2
        + [pltpu.VMEM((2 * count, LANES), F32)],
        compiler_params=params(48),
        name="add_rows",
        cost_estimate=pl.CostEstimate(flops=0, bytes_accessed=0, transcendentals=0),
    )(*plan, given)


def spread_body(pairs, *refs):
    for i in range(pairs):
        counts_ref, part_ref, out_ref = refs[2 * i], refs[2 * i + 1], refs[2 * pairs + i]
        out_ref[...] = left_product(counts_ref[...], part_ref[...]).astype(BF)


def spread_call(counts, parts, steps):
    n, feat = parts[0].shape
    specs, args = [], []
    for c, p in zip(counts, parts):
        specs += [
            pl.BlockSpec((n, c.shape[1] // steps), lambda i: (0, i)),
            pl.BlockSpec(p.shape, lambda i: (0, 0)),
        ]
        args += [c, p]
    return pl.pallas_call(
        functools.partial(spread_body, len(counts)),
        grid=(steps,),
        in_specs=specs,
        out_specs=[pl.BlockSpec((c.shape[1] // steps, feat), lambda i: (i, 0)) for c in counts],
        out_shape=[jax.ShapeDtypeStruct((c.shape[1], feat), BF) for c in counts],
        compiler_params=params(48),
        name="spread",
    )(*args)


def widen_body(blocked, *refs):
    given, outs = refs[: blocked + 4], refs[blocked + 4 :]
    for x_ref, out_ref in zip(given[:blocked], outs[:blocked]):
        out_ref[...] = x_ref[...].astype(F32)
    own_ref, other_ref, first_ref, last_ref = given[blocked:]
    tail_ref, first_out_ref, last_out_ref, small_ref = outs[blocked:]
    tail_ref[...] = own_ref[...].astype(F32) + other_ref[...].astype(F32)

    @pl.when(pl.program_id(0) == 0)
    def _():
        rows = last_out_ref.shape[0]
        first_out_ref[...] = first_ref[...].astype(F32)
        last_out_ref[...] = last_ref[:rows, :].astype(F32)
        small_ref[...] = last_ref[rows:, :].astype(F32)


def widen_call(arrays, own, other, first, last, last_rows, steps):
    spec = lambda a: pl.BlockSpec((a.shape[0] // steps, a.shape[1]), lambda i: (i, 0))
    shapes = [a.shape for a in (*arrays, own, first)]
    shapes += [(last_rows, last.shape[1]), (last.shape[0] - last_rows, last.shape[1])]
    return pl.pallas_call(
        functools.partial(widen_body, len(arrays)),
        grid=(steps,),
        in_specs=[spec(a) for a in (*arrays, own, other)] + [whole_vmem()] * 2,
        out_specs=[spec(a) for a in (*arrays, own)] + [whole_vmem()] * 3,
        out_shape=[jax.ShapeDtypeStruct(s, F32) for s in shapes],
        compiler_params=params(48),
        name="widen",
    )(*arrays, own, other, first, last)


def softmax_body(
    inv_count,
    chunk,
    mask_ref,
    table_ref,
    table_t_ref,
    user_ref,
    user_t_ref,
    label_ref,
    d_user_t_ref,
    grad_ref,
    loss_ref,
    logits,
    grad_sum,
):
    rows, feat = table_ref.shape
    block = user_ref.shape[0]
    chunks = rows // chunk
    step = pl.program_id(0)

    @pl.when(step == 0)
    def _():
        grad_sum[...] = jnp.zeros(grad_sum.shape, F32)

    label = label_ref[...]
    user_t = user_t_ref[...]
    user = user_ref[...]
    iota = lax.broadcasted_iota(jnp.int32, (chunk, block), 0)

    def at(c):
        return pl.ds(pl.multiple_of(c * chunk, chunk), chunk)

    def fold(v, op):
        return op(v.reshape(chunk // 8, 8, block), axis=0)

    def first(c, carry):
        peak, pos = carry
        s = jnp.dot(table_ref[at(c), :], user_t, preferred_element_type=F32)
        pos = pos + fold(jnp.where(iota == label - c * chunk, s, 0.0), jnp.sum)
        s = s + jnp.concatenate([mask_ref[at(c), :]] * (block // LANES), axis=1)
        logits[at(c), :] = s
        return jnp.maximum(peak, fold(s, jnp.max)), pos

    peak, pos = lax.fori_loop(
        0,
        chunks,
        first,
        (jnp.full((8, block), -jnp.inf, F32), jnp.zeros((8, block), F32)),
    )
    pos = jnp.sum(pos, axis=0, keepdims=True)
    peak = jnp.maximum(jnp.max(peak, axis=0, keepdims=True), pos)

    def second(c, total):
        p = jnp.exp(logits[at(c), :] - peak)
        logits[at(c), :] = p
        return total + fold(p, jnp.sum)

    total = lax.fori_loop(0, chunks, second, jnp.zeros((8, block), F32))
    pos_exp = jnp.exp(pos - peak)
    total = jnp.sum(total, axis=0, keepdims=True) + pos_exp
    loss_ref[...] = peak + jnp.log(total) - pos
    scale = inv_count / total
    d_pos = (pos_exp / total - 1.0) * inv_count

    def third(c, d_user_t):
        d = logits[at(c), :] * scale
        d = jnp.where(iota == label - c * chunk, d + d_pos, d).astype(BF)
        grad_sum[at(c), :] += jnp.dot(d, user, preferred_element_type=F32)
        return d_user_t + jnp.dot(table_t_ref[:, at(c)], d, preferred_element_type=F32)

    d_user_t = lax.fori_loop(0, chunks, third, jnp.zeros((feat, block), F32))
    d_user_t_ref[...] = d_user_t.astype(BF)

    @pl.when(step == pl.num_programs(0) - 1)
    def _():
        grad_ref[...] = grad_sum[...].astype(BF)


def softmax_call(mask, table, user, labels, block=512, chunk=2048):
    n, feat = user.shape
    rows = table.shape[0]
    across = lambda h: pl.BlockSpec((h, block), lambda i: (0, i))
    return pl.pallas_call(
        functools.partial(softmax_body, 1.0 / n, chunk),
        grid=(n // block,),
        in_specs=[
            whole_vmem(),
            whole_vmem(),
            whole_vmem(),
            pl.BlockSpec((block, feat), lambda i: (i, 0)),
            across(feat),
            across(1),
        ],
        out_specs=[across(feat), whole_vmem(), across(1)],
        out_shape=[
            jax.ShapeDtypeStruct((feat, n), BF),
            jax.ShapeDtypeStruct((rows, feat), BF),
            jax.ShapeDtypeStruct((1, n), F32),
        ],
        scratch_shapes=[pltpu.VMEM((rows, block), F32), pltpu.VMEM((rows, feat), F32)],
        compiler_params=params(46),
        name="sampled_softmax",
    )(mask, table, table.T, user, user.T, labels.reshape(1, n))


def sampled_mask(negatives, rows):
    high = lax.broadcasted_iota(jnp.int32, (rows // LANES, negatives.shape[0]), 0)
    low = lax.broadcasted_iota(jnp.int32, (LANES, negatives.shape[0]), 0)
    high_hot = (high == negatives[None, :] // LANES).astype(BF)
    low_hot = (low == negatives[None, :] % LANES).astype(BF)
    sampled = right_product(high_hot, low_hot).reshape(rows, 1)
    return jnp.broadcast_to(jnp.where(sampled > 0.5, F32(0.0), F32(-1e30)), (rows, LANES))


def left_product(first_op, second_op):
    return lax.dot_general(
        first_op, second_op, (((0,), (0,)), ((), ())), preferred_element_type=F32
    )


def right_product(first_op, second_op):
    return lax.dot_general(
        first_op, second_op, (((1,), (1,)), ((), ())), preferred_element_type=F32
    )


def gelu_back(pre_value, d_act):
    unused, pull = jax.vjp(jax.nn.gelu, pre_value)
    return pull(d_act)[0]


def in_range_ids(ids, lengths, offset):
    slot = lax.broadcasted_iota(jnp.int32, ids.shape, 1)
    kept = jnp.where(slot < lengths[:, None], ids + offset, -1)
    return jnp.pad(kept, ((0, 0), (0, LANES // 2 - ids.shape[1])), constant_values=-1)


def local(
    hot_table,
    tail_table,
    word_table,
    out_table,
    w_first,
    b_first,
    w_second,
    b_second,
    w_third,
    b_third,
    dense_feats,
    hist_ids,
    hist_len,
    search_ids,
    search_len,
    requests,
    labels,
    negatives,
):
    feat = hot_table.shape[1]
    hot_rows = hot_table.shape[0]
    owners, per_owner = requests.shape
    slots = owners * per_owner
    examples_dev = hist_ids.shape[0]
    examples_all = examples_dev * lax.axis_size("group") * lax.axis_size("wide")
    shard_rows = tail_table.shape[0]
    hist_float = hist_len[:, None].astype(F32)
    search_float = search_len[:, None].astype(F32)

    asked = lax.all_to_all(requests, "wide", split_axis=0, concat_axis=0, tiled=True)
    asked = asked.reshape(slots)
    looked = gather_call(jnp.maximum(asked, 0), tail_table)
    returned = lax.all_to_all(
        looked.reshape(owners, per_owner, feat), "wide", split_axis=0, concat_axis=0, tiled=True
    ).reshape(slots, feat)

    ids = jnp.concatenate(
        [
            in_range_ids(hist_ids, hist_len, 0),
            in_range_ids(search_ids, search_len, hot_rows + slots),
        ],
        axis=1,
    )
    mask = sampled_mask(negatives, out_table.shape[0])
    unroll = 16
    plan = row_plan(asked, shard_rows, unroll)
    ids, mask, plan, looked = lax.optimization_barrier((ids, mask, plan, looked))
    hot_counts, slot_counts, word_counts, hot_sum, word_sum = counts_call(
        ids, hot_table, word_table, slots
    )

    hist_mean = (hot_sum + jnp.dot(slot_counts, returned, preferred_element_type=F32)) / hist_float
    search_mean = word_sum / search_float
    inputs = jnp.concatenate([hist_mean, search_mean, dense_feats.astype(F32)], axis=1).astype(BF)
    pre_first = jnp.dot(inputs, w_first, preferred_element_type=F32) + b_first.astype(F32)
    act_first = jax.nn.gelu(pre_first).astype(BF)
    pre_second = jnp.dot(act_first, w_second, preferred_element_type=F32) + b_second.astype(F32)
    act_second = jax.nn.gelu(pre_second).astype(BF)
    user = (jnp.dot(act_second, w_third, preferred_element_type=F32) + b_third.astype(F32)).astype(
        BF
    )

    d_user_t, out_grad, per_example = softmax_call(mask, out_table, user, labels)
    d_user = d_user_t.T
    d_pre_second = gelu_back(pre_second, right_product(d_user, w_third)).astype(BF)
    d_pre_first = gelu_back(pre_first, right_product(d_pre_second, w_second)).astype(BF)
    d_inputs = right_product(d_pre_first, w_first[: 2 * feat])
    hist_part = (d_inputs[:, :feat] / hist_float).astype(BF)
    word_part = (d_inputs[:, feat:] / search_float).astype(BF)

    hot_grad, word_grad = spread_call((hot_counts, word_counts), (hist_part, word_part), 4)
    w1_grad = left_product(inputs, d_pre_first).astype(BF)
    w2_grad = left_product(act_first, d_pre_second).astype(BF)
    w3_grad = left_product(act_second, d_user).astype(BF)
    small = [
        per_example,
        jnp.sum(d_pre_first.astype(F32), axis=0),
        jnp.sum(d_pre_second.astype(F32), axis=0),
        jnp.sum(d_user.astype(F32), axis=0),
    ]
    small_rows = jnp.concatenate([x.reshape(-1, feat) for x in small], axis=0).astype(BF)
    w3_rows = w3_grad.shape[0]
    small_rows = jnp.pad(small_rows, ((0, -small_rows.shape[0] % 16), (0, 0)))
    packed = (
        hot_grad,
        word_grad,
        out_grad,
        w1_grad,
        w2_grad,
        jnp.concatenate([w3_grad, small_rows], axis=0),
    )
    packed, hist_part = lax.optimization_barrier((packed, hist_part))
    summed = lax.psum(packed, ("group", "wide"))

    (slot_grad,) = spread_call((slot_counts,), (hist_part,), 4)
    owed = lax.all_to_all(
        slot_grad.reshape(owners, per_owner, feat), "wide", split_axis=0, concat_axis=0, tiled=True
    ).reshape(slots, feat)
    own = add_rows_call(plan, owed, shard_rows, unroll)
    other = lax.ppermute(own, "group", [(0, 1), (1, 0)])
    hot_all, word_all, out_all, w2_all, tail_grad, w1_all, w3_all, small_all = widen_call(
        (summed[0], summed[1], summed[2], summed[4]), own, other, summed[3], summed[5], w3_rows, 4
    )
    small_sums = []
    start = 0
    for x in small:
        small_sums.append(small_all[start : start + x.size // feat].reshape(-1))
        start += x.size // feat
    loss_all, b1_all, b2_all, b3_all = small_sums
    loss_value = jnp.sum(loss_all) / examples_all
    return (
        loss_value,
        hot_all,
        tail_grad,
        word_all,
        out_all,
        w1_all,
        b1_all,
        w2_all,
        b2_all,
        w3_all,
        b3_all,
    )


def solution(mesh):
    split = ("group", "wide")
    in_specs = (
        (P(), P("wide", None))
        + (P(),) * 8
        + (P(split, None), P(split, None), P(split), P(split, None), P(split), P(split, None))
        + (P(split), P())
    )
    out_specs = (P(), P(), P("wide", None)) + (P(),) * 8
    return jax.shard_map(local, mesh=mesh, in_specs=in_specs, out_specs=out_specs, check_vma=False)
```

```python
import functools

import jax
import jax.numpy as jnp
from jax import lax
from jax.experimental import pallas as pl
from jax.experimental.pallas import tpu as pltpu
from jax.sharding import PartitionSpec as P

BF = jnp.bfloat16
F32 = jnp.float32
LANES = 128
MIB = 1024 * 1024


def params(mib):
    return pltpu.CompilerParams(vmem_limit_bytes=mib * MIB)


def whole_vmem():
    return pl.BlockSpec(memory_space=pltpu.VMEM)


def whole_smem():
    return pl.BlockSpec(memory_space=pltpu.SMEM)


def counts_body(cuts, ids_ref, hot_ref, word_ref, *refs):
    count_refs = refs[: len(cuts)]
    hist_ref, word_sum_ref, scratch, low_ref, high_ref = refs[len(cuts) :]
    block = ids_ref.shape[0]
    groups = sum(cuts)
    rows = groups + 8
    ids = ids_ref[...]
    low_ref[...] = (ids & (LANES - 1)).astype(F32)
    place = lax.broadcasted_iota(jnp.int32, ids.shape, 0) & 7
    high_ref[...] = (jnp.where(ids < 0, -64, ids >> 7) + place).astype(F32)
    low_iota = lax.broadcasted_iota(jnp.int32, (LANES, LANES), 0).astype(BF)
    high_iota = lax.broadcasted_iota(jnp.int32, (rows, LANES), 0).astype(BF)
    one = jnp.ones((), BF)
    zero = jnp.zeros((), BF)
    unroll = block

    def build(i, carry):
        for k in range(unroll):
            e = i * unroll + k
            low = jnp.broadcast_to(low_ref[pl.ds(e, 1), :], (LANES, LANES)).astype(BF)
            high = jnp.broadcast_to(high_ref[pl.ds(e, 1), :], (rows, LANES)).astype(BF)
            low_hot = jnp.where(low_iota == low, one, zero)
            high_hot = jnp.where(high_iota == high, one, zero)
            scratch[pl.ds(pl.multiple_of(e * rows, 8), rows), :] = right_product(high_hot, low_hot)
        return carry

    lax.fori_loop(0, block // unroll, build, 0)

    def regroup(i, carry):
        here = pl.ds(pl.multiple_of(i * 32, 32), 32)
        g = 0
        for ref, cut in zip(count_refs, cuts):
            for c in range(cut):
                eights = [
                    scratch[pl.ds((i * 32 + e) * rows + g, 8, stride=rows + 1), :]
                    for e in range(0, 32, 8)
                ]
                ref[here, c * LANES : (c + 1) * LANES] = jnp.concatenate(eights, axis=0).astype(
                    jnp.int8
                )
                g += 1
        return carry

    lax.fori_loop(0, block // 32, regroup, 0)
    hist_ref[...] = jnp.dot(count_refs[0][...].astype(BF), hot_ref[...], preferred_element_type=F32)
    word_sum_ref[...] = jnp.dot(
        count_refs[-1][...].astype(BF), word_ref[...], preferred_element_type=F32
    )


def counts_call(ids, hot, word, tail_rows, block=128):
    n = ids.shape[0]
    feat = hot.shape[1]
    widths = (hot.shape[0], tail_rows, word.shape[0])
    cuts = tuple(w // LANES for w in widths)
    rows_of = lambda w: pl.BlockSpec((block, w), lambda i: (i, 0))
    fixed = lambda s: pl.BlockSpec(s, lambda i: (0, 0))
    return pl.pallas_call(
        functools.partial(counts_body, cuts),
        grid=(n // block,),
        in_specs=[rows_of(LANES), fixed(hot.shape), fixed(word.shape)],
        out_specs=[rows_of(w) for w in widths] + [rows_of(feat)] * 2,
        out_shape=[jax.ShapeDtypeStruct((n, w), jnp.int8) for w in widths]
        + [jax.ShapeDtypeStruct((n, feat), F32)] * 2,
        scratch_shapes=[pltpu.VMEM((block * (sum(cuts) + 8), LANES), F32)]
        + [pltpu.VMEM((block, LANES), F32)] * 2,
        compiler_params=params(56),
        name="counts",
    )(ids, hot, word)


def gather_body(unroll, ids_ref, table_ref, out_ref, wide, picked):
    rows = table_ref.shape[0]
    count = out_ref.shape[0]
    step = pl.program_id(0)

    @pl.when(step == 0)
    def _():
        def widen(i, carry):
            t = table_ref[pl.ds(pl.multiple_of(i * 128, 128), 128), :].astype(F32)
            wide[pl.ds(i * 256, 128, stride=2), :] = t[:, :LANES]
            wide[pl.ds(i * 256 + 1, 128, stride=2), :] = t[:, LANES:]
            return carry

        lax.fori_loop(0, rows // 128, widen, 0)

    def pick(i, carry):
        for k in range(unroll):
            at = i * unroll + k
            picked[pl.ds(at * 2, 2), :] = wide[pl.ds(ids_ref[step * count + at] * 2, 2), :]
        return carry

    lax.fori_loop(0, count // unroll, pick, 0)

    def join(i, carry):
        left = picked[pl.ds(i * 256, 128, stride=2), :]
        right = picked[pl.ds(i * 256 + 1, 128, stride=2), :]
        out_ref[pl.ds(pl.multiple_of(i * 128, 128), 128), :] = jnp.concatenate(
            [left, right], axis=1
        ).astype(BF)
        return carry

    lax.fori_loop(0, count // 128, join, 0)


def gather_call(ids, table, steps=1, unroll=64):
    rows, feat = table.shape
    count = ids.shape[0]
    return pl.pallas_call(
        functools.partial(gather_body, unroll),
        grid=(steps,),
        in_specs=[whole_smem(), whole_vmem()],
        out_specs=pl.BlockSpec((count // steps, feat), lambda i: (i, 0)),
        out_shape=jax.ShapeDtypeStruct((count, feat), BF),
        scratch_shapes=[
            pltpu.VMEM((2 * rows, LANES), F32),
            pltpu.VMEM((2 * count // steps, LANES), F32),
        ],
        compiler_params=params(60),
        name="gather_rows",
    )(ids, table)


def add_rows_body(unroll, ids_ref, again_ref, clash_ref, rows_ref, *refs):
    out_refs, (total_a, total_b, wide) = refs[:-3], refs[-3:]
    count = rows_ref.shape[0]
    part = out_refs[0].shape[0]
    rows = part * len(out_refs)

    def clear(i, carry):
        for total in (total_a, total_b):
            total[pl.ds(pl.multiple_of(i * 256, 256), 256), :] = jnp.zeros((256, LANES), F32)
        return carry

    lax.fori_loop(0, rows // 128, clear, 0)

    def widen(i, carry):
        t = rows_ref[pl.ds(pl.multiple_of(i * 128, 128), 128), :].astype(F32)
        wide[pl.ds(i * 256, 128, stride=2), :] = t[:, :LANES]
        wide[pl.ds(i * 256 + 1, 128, stride=2), :] = t[:, LANES:]
        return carry

    lax.fori_loop(0, count // 128, widen, 0)

    def given(at):
        return wide[pl.ds(at * 2, 2), :]

    def add(i, carry):
        for total, base in ((total_a, i * 2 * unroll), (total_b, (i * 2 + 1) * unroll)):
            places = [pl.ds(ids_ref[base + k] * 2, 2) for k in range(unroll)]
            sums = [total[p, :] + given(base + k) for k, p in enumerate(places)]
            for p, v in zip(places, sums):
                total[p, :] = v
        return carry

    lax.fori_loop(0, count // (2 * unroll), add, 0)

    groups = count // unroll
    section = 16

    def check(i, carry):
        @pl.when(clash_ref[groups + i] != 0)
        def _():
            def add_again(j, inner):
                group = i * section + j

                @pl.when(clash_ref[group] != 0)
                def _():
                    for k in range(unroll):
                        p = pl.ds(again_ref[group * unroll + k] * 2, 2)
                        total_a[p, :] = total_a[p, :] + given(group * unroll + k)

                return inner

            lax.fori_loop(0, section, add_again, 0)

        return carry

    lax.fori_loop(0, groups // section, check, 0)

    for n, out_ref in enumerate(out_refs):

        def join(i, carry, n=n, out_ref=out_ref):
            left = pl.ds(n * part * 2 + i * 256, 128, stride=2)
            right = pl.ds(n * part * 2 + i * 256 + 1, 128, stride=2)
            both = [total_a[p, :] + total_b[p, :] for p in (left, right)]
            here = pl.ds(pl.multiple_of(i * 128, 128), 128)
            out_ref[here, :] = jnp.concatenate(both, axis=1).astype(out_ref.dtype)
            return carry

        lax.fori_loop(0, part // 128, join, 0)


def row_plan(ids, rows, unroll):
    grouped = ids.reshape(-1, unroll)
    spare = rows + lax.broadcasted_iota(jnp.int32, grouped.shape, 1)
    earlier = lax.broadcasted_iota(jnp.int32, (unroll, unroll), 1) < lax.broadcasted_iota(
        jnp.int32, (unroll, unroll), 0
    )
    same = (grouped[:, :, None] == grouped[:, None, :]) & earlier[None]
    twice = jnp.any(same, axis=2) & (grouped >= 0)
    once = jnp.where((grouped >= 0) & ~twice, grouped, spare)
    again = jnp.where(twice, grouped, spare)
    clash = jnp.any(twice, axis=1).astype(jnp.int32)
    sections = jnp.max(clash.reshape(-1, 16), axis=1)
    return once.reshape(-1), again.reshape(-1), jnp.concatenate([clash, sections])


def add_rows_call(plan, given, rows, unroll, parts):
    count, feat = given.shape
    return pl.pallas_call(
        functools.partial(add_rows_body, unroll),
        in_specs=[whole_smem()] * 3 + [whole_vmem()],
        out_specs=[whole_vmem()] * parts,
        out_shape=[jax.ShapeDtypeStruct((rows // parts, feat), BF)] * parts,
        scratch_shapes=[pltpu.VMEM((2 * (rows + unroll), LANES), F32)] * 2
        + [pltpu.VMEM((2 * count, LANES), F32)],
        compiler_params=params(48),
        name="add_rows",
        cost_estimate=pl.CostEstimate(flops=0, bytes_accessed=0, transcendentals=0),
    )(*plan, given)


def spread_body(pairs, *refs):
    for i in range(pairs):
        counts_ref, part_ref, out_ref = refs[2 * i], refs[2 * i + 1], refs[2 * pairs + i]
        out_ref[...] = left_product(counts_ref[...].astype(BF), part_ref[...]).astype(BF)


def spread_call(counts, parts, steps):
    n, feat = parts[0].shape
    specs, args = [], []
    for c, p in zip(counts, parts):
        specs += [pl.BlockSpec((n, c.shape[1] // steps), lambda i: (0, i)), whole_vmem()]
        args += [c, p]
    return pl.pallas_call(
        functools.partial(spread_body, len(counts)),
        grid=(steps,),
        in_specs=specs,
        out_specs=[pl.BlockSpec((c.shape[1] // steps, feat), lambda i: (i, 0)) for c in counts],
        out_shape=[jax.ShapeDtypeStruct((c.shape[1], feat), BF) for c in counts],
        compiler_params=params(60),
        name="spread",
    )(*args)


def widen_body(blocked, *refs):
    given, outs = refs[: blocked + 2], refs[blocked + 2 :]
    for x_ref, out_ref in zip(given[:blocked], outs[:blocked]):
        out_ref[...] = x_ref[...].astype(F32)
    first_ref, last_ref = given[blocked:]
    first_out_ref, last_out_ref, loss_ref, *bias_refs = outs[blocked:]

    @pl.when(pl.program_id(0) == 0)
    def _():
        rows, feat = last_out_ref.shape
        first_out_ref[...] = first_ref[...].astype(F32)
        last_out_ref[...] = last_ref[:rows, :].astype(F32)
        small = last_ref[rows:, :].astype(F32)
        start = loss_ref.shape[0]
        loss_ref[...] = small[:start]
        for ref in bias_refs:
            for i in range(ref.shape[1] // feat):
                ref[:, i * feat : (i + 1) * feat] = small[start : start + 1]
                start += 1


def widen_call(arrays, first, last, last_rows, loss_rows, widths, steps):
    feat = last.shape[1]
    spec = lambda a: pl.BlockSpec((a.shape[0] // steps, a.shape[1]), lambda i: (i, 0))
    shapes = [a.shape for a in (*arrays, first)] + [(last_rows, feat), (loss_rows, feat)]
    shapes += [(1, w) for w in widths]
    return pl.pallas_call(
        functools.partial(widen_body, len(arrays)),
        grid=(steps,),
        in_specs=[spec(a) for a in arrays] + [whole_vmem()] * 2,
        out_specs=[spec(a) for a in arrays] + [whole_vmem()] * (len(shapes) - len(arrays)),
        out_shape=[jax.ShapeDtypeStruct(s, F32) for s in shapes],
        compiler_params=params(60),
        name="widen",
    )(*arrays, first, last)


def add_parts_body(*refs):
    count = len(refs) // 2
    for k in range(count):

        @pl.when(pl.program_id(0) == k)
        def _(k=k):
            refs[-1][...] = refs[k][...].astype(F32) + refs[count + k][...].astype(F32)


def add_pair_call(own, others):
    rows, feat = own[0].shape
    spec = pl.BlockSpec((rows, feat), lambda i: (0, 0))
    return pl.pallas_call(
        add_parts_body,
        grid=(len(own),),
        in_specs=[spec] * (2 * len(own)),
        out_specs=pl.BlockSpec((rows, feat), lambda i: (i, 0)),
        out_shape=jax.ShapeDtypeStruct((rows * len(own), feat), F32),
        compiler_params=params(60),
        cost_estimate=pl.CostEstimate(flops=0, bytes_accessed=0, transcendentals=0),
        name="add_parts",
    )(*own, *others)


def softmax_body(
    inv_count,
    chunk,
    mask_ref,
    table_ref,
    table_t_ref,
    user_ref,
    user_t_ref,
    label_ref,
    d_user_t_ref,
    grad_ref,
    loss_ref,
    logits,
    grad_sum,
):
    rows, feat = table_ref.shape
    block = user_ref.shape[0]
    chunks = rows // chunk
    step = pl.program_id(0)

    @pl.when(step == 0)
    def _():
        grad_sum[...] = jnp.zeros(grad_sum.shape, F32)

    label = label_ref[...]
    user_t = user_t_ref[...]
    user = user_ref[...]
    iota = lax.broadcasted_iota(jnp.int32, (chunk, block), 0)

    def at(c):
        return pl.ds(pl.multiple_of(c * chunk, chunk), chunk)

    def fold(v, op):
        return op(v.reshape(chunk // 8, 8, block), axis=0)

    def first(c, carry):
        peak, pos = carry
        s = jnp.dot(table_ref[at(c), :], user_t, preferred_element_type=F32)
        pos = pos + fold(jnp.where(iota == label - c * chunk, s, 0.0), jnp.sum)
        s = s + jnp.concatenate([mask_ref[at(c), :]] * (block // LANES), axis=1)
        logits[at(c), :] = s
        return jnp.maximum(peak, fold(s, jnp.max)), pos

    peak, pos = lax.fori_loop(
        0,
        chunks,
        first,
        (jnp.full((8, block), -jnp.inf, F32), jnp.zeros((8, block), F32)),
    )
    pos = jnp.sum(pos, axis=0, keepdims=True)
    peak = jnp.maximum(jnp.max(peak, axis=0, keepdims=True), pos)

    def second(c, total):
        p = jnp.exp(logits[at(c), :] - peak)
        logits[at(c), :] = p
        return total + fold(p, jnp.sum)

    total = lax.fori_loop(0, chunks, second, jnp.zeros((8, block), F32))
    pos_exp = jnp.exp(pos - peak)
    total = jnp.sum(total, axis=0, keepdims=True) + pos_exp
    loss_ref[...] = peak + jnp.log(total) - pos
    scale = inv_count / total
    d_pos = (pos_exp / total - 1.0) * inv_count

    def third(c, d_user_t):
        d = logits[at(c), :] * scale
        d = jnp.where(iota == label - c * chunk, d + d_pos, d).astype(BF)
        grad_sum[at(c), :] += jnp.dot(d, user, preferred_element_type=F32)
        return d_user_t + jnp.dot(table_t_ref[:, at(c)], d, preferred_element_type=F32)

    d_user_t = lax.fori_loop(0, chunks, third, jnp.zeros((feat, block), F32))
    d_user_t_ref[...] = d_user_t.astype(BF)

    @pl.when(step == pl.num_programs(0) - 1)
    def _():
        grad_ref[...] = grad_sum[...].astype(BF)


def softmax_call(mask, table, table_t, user, labels, block=512, chunk=2048):
    n, feat = user.shape
    rows = table.shape[0]
    across = lambda h: pl.BlockSpec((h, block), lambda i: (0, i))
    return pl.pallas_call(
        functools.partial(softmax_body, 1.0 / n, chunk),
        grid=(n // block,),
        in_specs=[
            whole_vmem(),
            whole_vmem(),
            whole_vmem(),
            pl.BlockSpec((block, feat), lambda i: (i, 0)),
            across(feat),
            across(1),
        ],
        out_specs=[across(feat), whole_vmem(), across(1)],
        out_shape=[
            jax.ShapeDtypeStruct((feat, n), BF),
            jax.ShapeDtypeStruct((rows, feat), BF),
            jax.ShapeDtypeStruct((1, n), F32),
        ],
        scratch_shapes=[pltpu.VMEM((rows, block), F32), pltpu.VMEM((rows, feat), F32)],
        compiler_params=params(46),
        name="sampled_softmax",
    )(mask, table, table_t, user, user.T, labels.reshape(1, n))


def sampled_mask(negatives, rows):
    high = lax.broadcasted_iota(jnp.int32, (rows // LANES, negatives.shape[0]), 0)
    low = lax.broadcasted_iota(jnp.int32, (LANES, negatives.shape[0]), 0)
    high_hot = (high == negatives[None, :] // LANES).astype(BF)
    low_hot = (low == negatives[None, :] % LANES).astype(BF)
    sampled = right_product(high_hot, low_hot).reshape(rows, 1)
    return jnp.broadcast_to(jnp.where(sampled > 0.5, F32(0.0), F32(-1e30)), (rows, LANES))


def left_product(first_op, second_op):
    return lax.dot_general(
        first_op, second_op, (((0,), (0,)), ((), ())), preferred_element_type=F32
    )


def right_product(first_op, second_op):
    return lax.dot_general(
        first_op, second_op, (((1,), (1,)), ((), ())), preferred_element_type=F32
    )


def gelu_back(pre_value, d_act):
    unused, pull = jax.vjp(jax.nn.gelu, pre_value)
    return pull(d_act)[0]


def in_range_ids(ids, lengths, offset):
    slot = lax.broadcasted_iota(jnp.int32, ids.shape, 1)
    kept = jnp.where(slot < lengths[:, None], ids + offset, -1)
    return jnp.pad(kept, ((0, 0), (0, LANES // 2 - ids.shape[1])), constant_values=-1)


def local(
    hot_table,
    tail_table,
    word_table,
    out_table,
    w_first,
    b_first,
    w_second,
    b_second,
    w_third,
    b_third,
    dense_feats,
    hist_ids,
    hist_len,
    search_ids,
    search_len,
    requests,
    labels,
    negatives,
):
    feat = hot_table.shape[1]
    hot_rows = hot_table.shape[0]
    owners, per_owner = requests.shape
    slots = owners * per_owner
    examples_dev = hist_ids.shape[0]
    examples_all = examples_dev * lax.axis_size("group") * lax.axis_size("wide")
    shard_rows = tail_table.shape[0]
    hist_float = hist_len[:, None].astype(F32)
    search_float = search_len[:, None].astype(F32)

    asked = lax.all_to_all(requests, "wide", split_axis=0, concat_axis=0, tiled=True)
    asked = asked.reshape(slots)
    looked = gather_call(jnp.maximum(asked, 0), tail_table)
    returned = lax.all_to_all(
        looked.reshape(owners, per_owner, feat), "wide", split_axis=0, concat_axis=0, tiled=True
    ).reshape(slots, feat)

    asked, negatives, looked = lax.optimization_barrier((asked, negatives, looked))
    ids = jnp.concatenate(
        [
            in_range_ids(hist_ids, hist_len, 0),
            in_range_ids(search_ids, search_len, hot_rows + slots),
        ],
        axis=1,
    )
    out_table_t = out_table.T
    mask = sampled_mask(negatives, out_table.shape[0])
    unroll = 16
    plan = row_plan(asked, shard_rows, unroll)
    ids, out_table_t, mask, plan, looked = lax.optimization_barrier(
        (ids, out_table_t, mask, plan, looked)
    )
    hot_counts, slot_counts, word_counts, hot_sum, word_sum = counts_call(
        ids, hot_table, word_table, slots
    )

    hist_mean = (hot_sum + jnp.dot(slot_counts.astype(BF), returned, preferred_element_type=F32)) / hist_float
    search_mean = word_sum / search_float
    inputs = jnp.concatenate([hist_mean, search_mean, dense_feats.astype(F32)], axis=1).astype(BF)
    pre_first = jnp.dot(inputs, w_first, preferred_element_type=F32) + b_first.astype(F32)
    act_first = jax.nn.gelu(pre_first).astype(BF)
    pre_second = jnp.dot(act_first, w_second, preferred_element_type=F32) + b_second.astype(F32)
    act_second = jax.nn.gelu(pre_second).astype(BF)
    user = (jnp.dot(act_second, w_third, preferred_element_type=F32) + b_third.astype(F32)).astype(
        BF
    )

    d_user_t, out_grad, per_example = softmax_call(mask, out_table, out_table_t, user, labels)
    d_user = d_user_t.T
    d_pre_second = gelu_back(pre_second, right_product(d_user, w_third)).astype(BF)
    d_pre_first = gelu_back(pre_first, right_product(d_pre_second, w_second)).astype(BF)
    d_inputs = right_product(d_pre_first, w_first[: 2 * feat])
    hist_part = (d_inputs[:, :feat] / hist_float).astype(BF)
    word_part = (d_inputs[:, feat:] / search_float).astype(BF)

    hot_grad, word_grad = spread_call((hot_counts, word_counts), (hist_part, word_part), 4)
    w1_grad = left_product(inputs, d_pre_first).astype(BF)
    w2_grad = left_product(act_first, d_pre_second).astype(BF)
    w3_grad = left_product(act_second, d_user).astype(BF)
    small = [
        per_example,
        jnp.sum(d_pre_first.astype(F32), axis=0),
        jnp.sum(d_pre_second.astype(F32), axis=0),
        jnp.sum(d_user.astype(F32), axis=0),
    ]
    small_rows = jnp.concatenate([x.reshape(-1, feat) for x in small], axis=0).astype(BF)
    w3_rows = w3_grad.shape[0]
    small_rows = jnp.pad(small_rows, ((0, -small_rows.shape[0] % 16), (0, 0)))
    packed = (
        hot_grad,
        word_grad,
        out_grad,
        w1_grad,
        w2_grad,
        jnp.concatenate([w3_grad, small_rows], axis=0),
    )
    packed, hist_part = lax.optimization_barrier((packed, hist_part))
    summed = lax.psum(packed, ("group", "wide"))

    (slot_grad,) = spread_call((slot_counts,), (hist_part,), 4)
    owed = lax.all_to_all(
        slot_grad.reshape(owners, per_owner, feat), "wide", split_axis=0, concat_axis=0, tiled=True
    ).reshape(slots, feat)
    own = add_rows_call(plan, owed, shard_rows, unroll, 4)
    others = [lax.ppermute(x, "group", [(0, 1), (1, 0)]) for x in own]
    tail_grad = add_pair_call(own, others)
    summed, tail_grad = lax.optimization_barrier((summed, tail_grad))
    hot_all, word_all, out_all, w2_all, w1_all, w3_all, losses, b1_all, b2_all, b3_all = widen_call(
        (summed[0], summed[1], summed[2], summed[4]),
        summed[3],
        summed[5],
        w3_rows,
        examples_dev // feat,
        (b_first.shape[0], b_second.shape[0], b_third.shape[0]),
        4,
    )
    loss_value = jnp.sum(losses) / examples_all
    return (
        loss_value,
        hot_all,
        tail_grad,
        word_all,
        out_all,
        w1_all,
        b1_all[0],
        w2_all,
        b2_all[0],
        w3_all,
        b3_all[0],
    )


def solution(mesh):
    split = ("group", "wide")
    in_specs = (
        (P(), P("wide", None))
        + (P(),) * 8
        + (P(split, None), P(split, None), P(split), P(split, None), P(split), P(split, None))
        + (P(split), P())
    )
    out_specs = (P(), P(), P("wide", None)) + (P(),) * 8
    return jax.shard_map(local, mesh=mesh, in_specs=in_specs, out_specs=out_specs, check_vma=False)
```

```python
import functools

import jax
import jax.numpy as jnp
from jax import lax
from jax.experimental import pallas as pl
from jax.experimental.pallas import tpu as pltpu
from jax.sharding import PartitionSpec as P

BF = jnp.bfloat16
F32 = jnp.float32
LANES = 128
MIB = 1024 * 1024


def params(mib):
    return pltpu.CompilerParams(vmem_limit_bytes=mib * MIB)


def whole_vmem():
    return pl.BlockSpec(memory_space=pltpu.VMEM)


def whole_smem():
    return pl.BlockSpec(memory_space=pltpu.SMEM)


def counts_body(cuts, ids_ref, hot_ref, word_ref, *refs):
    count_refs = refs[: len(cuts)]
    hist_ref, word_sum_ref, scratch, low_ref, high_ref = refs[len(cuts) :]
    block = ids_ref.shape[0]
    groups = sum(cuts)
    rows = groups + 8
    ids = ids_ref[...]
    low_ref[...] = (ids & (LANES - 1)).astype(F32)
    place = lax.broadcasted_iota(jnp.int32, ids.shape, 0) & 7
    high_ref[...] = (jnp.where(ids < 0, -64, ids >> 7) + place).astype(F32)
    low_iota = lax.broadcasted_iota(jnp.int32, (LANES, LANES), 0).astype(BF)
    high_iota = lax.broadcasted_iota(jnp.int32, (rows, LANES), 0).astype(BF)
    one = jnp.ones((), BF)
    zero = jnp.zeros((), BF)
    unroll = block

    def build(i, carry):
        for k in range(unroll):
            e = i * unroll + k
            low = jnp.broadcast_to(low_ref[pl.ds(e, 1), :], (LANES, LANES)).astype(BF)
            high = jnp.broadcast_to(high_ref[pl.ds(e, 1), :], (rows, LANES)).astype(BF)
            low_hot = jnp.where(low_iota == low, one, zero)
            high_hot = jnp.where(high_iota == high, one, zero)
            scratch[pl.ds(pl.multiple_of(e * rows, 8), rows), :] = right_product(high_hot, low_hot)
        return carry

    lax.fori_loop(0, block // unroll, build, 0)

    def regroup(i, carry):
        here = pl.ds(pl.multiple_of(i * 32, 32), 32)
        g = 0
        for ref, cut in zip(count_refs, cuts):
            for c in range(cut):
                eights = [
                    scratch[pl.ds((i * 32 + e) * rows + g, 8, stride=rows + 1), :]
                    for e in range(0, 32, 8)
                ]
                ref[here, c * LANES : (c + 1) * LANES] = jnp.concatenate(eights, axis=0).astype(
                    jnp.int8
                )
                g += 1
        return carry

    lax.fori_loop(0, block // 32, regroup, 0)
    hist_ref[...] = jnp.dot(count_refs[0][...].astype(BF), hot_ref[...], preferred_element_type=F32)
    word_sum_ref[...] = jnp.dot(
        count_refs[-1][...].astype(BF), word_ref[...], preferred_element_type=F32
    )


def counts_call(ids, hot, word, tail_rows, block=128):
    n = ids.shape[0]
    feat = hot.shape[1]
    widths = (hot.shape[0], tail_rows, word.shape[0])
    cuts = tuple(w // LANES for w in widths)
    rows_of = lambda w: pl.BlockSpec((block, w), lambda i: (i, 0))
    fixed = lambda s: pl.BlockSpec(s, lambda i: (0, 0))
    return pl.pallas_call(
        functools.partial(counts_body, cuts),
        grid=(n // block,),
        in_specs=[rows_of(LANES), fixed(hot.shape), fixed(word.shape)],
        out_specs=[rows_of(w) for w in widths] + [rows_of(feat)] * 2,
        out_shape=[jax.ShapeDtypeStruct((n, w), jnp.int8) for w in widths]
        + [jax.ShapeDtypeStruct((n, feat), F32)] * 2,
        scratch_shapes=[pltpu.VMEM((block * (sum(cuts) + 8), LANES), F32)]
        + [pltpu.VMEM((block, LANES), F32)] * 2,
        compiler_params=params(56),
        name="counts",
    )(ids, hot, word)


def gather_body(parts, ids_ref, table_hbm, out_hbm, table, wide, picked, out, sems):
    rows = table.shape[0]
    owners, each = ids_ref.shape
    here = lambda i, size: pl.ds(pl.multiple_of(i * size, size), size)
    given = rows // parts
    taken = owners // parts
    inward = [
        pltpu.make_async_copy(
            table_hbm.at[here(p, given)], table.at[here(p, given)], sems.at[0, p]
        )
        for p in range(parts)
    ]
    outward = [
        pltpu.make_async_copy(
            out.at[here(p, taken * each)], out_hbm.at[here(p, taken * each)], sems.at[1, p]
        )
        for p in range(parts)
    ]
    for copy in inward:
        copy.start()
    wide[:8, :] = jnp.zeros((8, LANES), F32)
    for p in range(parts):
        inward[p].wait()

        def widen(i, carry, p=p):
            i = i + p * (given // 128)
            t = table[here(i, 128), :].astype(F32)
            wide[pl.ds(8 + i * 256, 128, stride=2), :] = t[:, :LANES]
            wide[pl.ds(9 + i * 256, 128, stride=2), :] = t[:, LANES:]
            return carry

        lax.fori_loop(0, given // 128, widen, 0)

    for p in range(parts):

        def pick(owner, carry):
            for k in range(each):
                at = owner * each + k
                picked[pl.ds(at * 2, 2), :] = wide[pl.ds(ids_ref[owner, k] * 2 + 8, 2), :]
            return carry

        lax.fori_loop(p * taken, (p + 1) * taken, pick, 0)

        def join(i, carry):
            left = picked[pl.ds(i * 256, 128, stride=2), :]
            right = picked[pl.ds(i * 256 + 1, 128, stride=2), :]
            out[here(i, 128), :] = jnp.concatenate([left, right], axis=1).astype(BF)
            return carry

        lax.fori_loop(p * taken * each // 128, (p + 1) * taken * each // 128, join, 0)
        outward[p].start()
    for copy in outward:
        copy.wait()


def gather_call(ids, table, parts=8):
    rows, feat = table.shape
    count = ids.size
    return pl.pallas_call(
        functools.partial(gather_body, parts),
        in_specs=[whole_smem(), pl.BlockSpec(memory_space=pl.ANY)],
        out_specs=pl.BlockSpec(memory_space=pl.ANY),
        out_shape=jax.ShapeDtypeStruct((count, feat), BF),
        scratch_shapes=[
            pltpu.VMEM((rows, feat), BF),
            pltpu.VMEM((2 * rows + 8, LANES), F32),
            pltpu.VMEM((2 * count, LANES), F32),
            pltpu.VMEM((count, feat), BF),
            pltpu.SemaphoreType.DMA((2, parts)),
        ],
        compiler_params=params(60),
        name="gather_rows",
    )(ids, table)


def add_rows_body(unroll, ids_ref, again_ref, clash_ref, rows_ref, *refs):
    out_refs, (total_a, total_b, wide) = refs[:-3], refs[-3:]
    count = rows_ref.shape[0]
    part = out_refs[0].shape[0]
    rows = part * len(out_refs)

    def clear(i, carry):
        for total in (total_a, total_b):
            total[pl.ds(pl.multiple_of(i * 256, 256), 256), :] = jnp.zeros((256, LANES), F32)
        return carry

    lax.fori_loop(0, rows // 128, clear, 0)

    def widen(i, carry):
        t = rows_ref[pl.ds(pl.multiple_of(i * 128, 128), 128), :].astype(F32)
        wide[pl.ds(i * 256, 128, stride=2), :] = t[:, :LANES]
        wide[pl.ds(i * 256 + 1, 128, stride=2), :] = t[:, LANES:]
        return carry

    lax.fori_loop(0, count // 128, widen, 0)

    def given(at):
        return wide[pl.ds(at * 2, 2), :]

    def add(i, carry):
        for total, base in ((total_a, i * 2 * unroll), (total_b, (i * 2 + 1) * unroll)):
            places = [pl.ds(ids_ref[base + k] * 2, 2) for k in range(unroll)]
            sums = [total[p, :] + given(base + k) for k, p in enumerate(places)]
            for p, v in zip(places, sums):
                total[p, :] = v
        return carry

    lax.fori_loop(0, count // (2 * unroll), add, 0)

    groups = count // unroll
    section = 16

    def check(i, carry):
        @pl.when(clash_ref[groups + i] != 0)
        def _():
            def add_again(j, inner):
                group = i * section + j

                @pl.when(clash_ref[group] != 0)
                def _():
                    for k in range(unroll):
                        p = pl.ds(again_ref[group * unroll + k] * 2, 2)
                        total_a[p, :] = total_a[p, :] + given(group * unroll + k)

                return inner

            lax.fori_loop(0, section, add_again, 0)

        return carry

    lax.fori_loop(0, groups // section, check, 0)

    for n, out_ref in enumerate(out_refs):

        def join(i, carry, n=n, out_ref=out_ref):
            left = pl.ds(n * part * 2 + i * 256, 128, stride=2)
            right = pl.ds(n * part * 2 + i * 256 + 1, 128, stride=2)
            both = [total_a[p, :] + total_b[p, :] for p in (left, right)]
            here = pl.ds(pl.multiple_of(i * 128, 128), 128)
            out_ref[here, :] = jnp.concatenate(both, axis=1).astype(out_ref.dtype)
            return carry

        lax.fori_loop(0, part // 128, join, 0)


def row_plan(ids, rows, unroll):
    grouped = ids.reshape(-1, unroll)
    spare = rows + lax.broadcasted_iota(jnp.int32, grouped.shape, 1)
    earlier = lax.broadcasted_iota(jnp.int32, (unroll, unroll), 1) < lax.broadcasted_iota(
        jnp.int32, (unroll, unroll), 0
    )
    same = (grouped[:, :, None] == grouped[:, None, :]) & earlier[None]
    twice = jnp.any(same, axis=2) & (grouped >= 0)
    once = jnp.where((grouped >= 0) & ~twice, grouped, spare)
    again = jnp.where(twice, grouped, spare)
    clash = jnp.any(twice, axis=1).astype(jnp.int32)
    sections = jnp.max(clash.reshape(-1, 16), axis=1)
    return once.reshape(-1), again.reshape(-1), jnp.concatenate([clash, sections])


def add_rows_call(plan, given, rows, unroll, parts):
    count, feat = given.shape
    return pl.pallas_call(
        functools.partial(add_rows_body, unroll),
        in_specs=[whole_smem()] * 3 + [whole_vmem()],
        out_specs=[whole_vmem()] * parts,
        out_shape=[jax.ShapeDtypeStruct((rows // parts, feat), BF)] * parts,
        scratch_shapes=[pltpu.VMEM((2 * (rows + unroll), LANES), F32)] * 2
        + [pltpu.VMEM((2 * count, LANES), F32)],
        compiler_params=params(48),
        name="add_rows",
        cost_estimate=pl.CostEstimate(flops=0, bytes_accessed=0, transcendentals=0),
    )(*plan, given)


def spread_body(pairs, firsts, d_inputs_ref, *refs):
    part_refs = refs[3 * pairs :]
    feat = part_refs[0].shape[1]

    @pl.when(pl.program_id(0) == 0)
    def _():
        for i, first in enumerate(firsts):
            d_mean = d_inputs_ref[:, first : first + feat]
            part_refs[i][...] = (d_mean / refs[2 * i + 1][...]).astype(BF)

    for i in range(pairs):
        counts_ref, out_ref = refs[2 * i], refs[2 * pairs + i]
        out_ref[...] = left_product(counts_ref[...].astype(BF), part_refs[i][...]).astype(BF)


def spread_call(counts, lengths, d_inputs, firsts, feat, steps):
    n = d_inputs.shape[0]
    specs, args = [whole_vmem()], [d_inputs]
    for c, x in zip(counts, lengths):
        specs += [pl.BlockSpec((n, c.shape[1] // steps), lambda i: (0, i)), whole_vmem()]
        args += [c, x]
    return pl.pallas_call(
        functools.partial(spread_body, len(counts), firsts),
        grid=(steps,),
        in_specs=specs,
        out_specs=[pl.BlockSpec((c.shape[1] // steps, feat), lambda i: (i, 0)) for c in counts],
        out_shape=[jax.ShapeDtypeStruct((c.shape[1], feat), BF) for c in counts],
        scratch_shapes=[pltpu.VMEM((n, feat), BF)] * len(counts),
        compiler_params=params(60),
        name="spread",
    )(*args)


def widen_body(blocked, *refs):
    given, outs = refs[: blocked + 2], refs[blocked + 2 :]
    for x_ref, out_ref in zip(given[:blocked], outs[:blocked]):
        out_ref[...] = x_ref[...].astype(F32)
    first_ref, last_ref = given[blocked:]
    first_out_ref, last_out_ref, loss_ref, *bias_refs = outs[blocked:]

    @pl.when(pl.program_id(0) == 0)
    def _():
        rows, feat = last_out_ref.shape
        first_out_ref[...] = first_ref[...].astype(F32)
        last_out_ref[...] = last_ref[:rows, :].astype(F32)
        small = last_ref[rows:, :].astype(F32)
        start = loss_ref.shape[0]
        loss_ref[...] = small[:start]
        for ref in bias_refs:
            for i in range(ref.shape[1] // feat):
                ref[:, i * feat : (i + 1) * feat] = small[start : start + 1]
                start += 1


def widen_call(arrays, first, last, last_rows, loss_rows, widths, steps):
    feat = last.shape[1]
    spec = lambda a: pl.BlockSpec((a.shape[0] // steps, a.shape[1]), lambda i: (i, 0))
    shapes = [a.shape for a in (*arrays, first)] + [(last_rows, feat), (loss_rows, feat)]
    shapes += [(1, w) for w in widths]
    return pl.pallas_call(
        functools.partial(widen_body, len(arrays)),
        grid=(steps,),
        in_specs=[spec(a) for a in arrays] + [whole_vmem()] * 2,
        out_specs=[spec(a) for a in arrays] + [whole_vmem()] * (len(shapes) - len(arrays)),
        out_shape=[jax.ShapeDtypeStruct(s, F32) for s in shapes],
        compiler_params=params(60),
        name="widen",
    )(*arrays, first, last)


def add_parts_body(*refs):
    count = len(refs) // 2
    for k in range(count):

        @pl.when(pl.program_id(0) == k)
        def _(k=k):
            refs[-1][...] = refs[k][...].astype(F32) + refs[count + k][...].astype(F32)


def add_pair_call(own, others):
    rows, feat = own[0].shape
    spec = pl.BlockSpec((rows, feat), lambda i: (0, 0))
    return pl.pallas_call(
        add_parts_body,
        grid=(len(own),),
        in_specs=[spec] * (2 * len(own)),
        out_specs=pl.BlockSpec((rows, feat), lambda i: (i, 0)),
        out_shape=jax.ShapeDtypeStruct((rows * len(own), feat), F32),
        compiler_params=params(60),
        cost_estimate=pl.CostEstimate(flops=0, bytes_accessed=0, transcendentals=0),
        name="add_parts",
    )(*own, *others)


def softmax_body(
    inv_count,
    chunk,
    mask_hbm,
    table_hbm,
    table_t_hbm,
    user_t_ref,
    label_ref,
    d_user_t_ref,
    grad_ref,
    loss_ref,
    logits,
    grad_sum,
    mask_ref,
    table_ref,
    table_t_ref,
    sems,
):
    rows, feat = table_ref.shape
    block = user_t_ref.shape[1]
    chunks = rows // chunk
    step = pl.program_id(0)
    last = pl.num_programs(0) - 1

    def at(c):
        return pl.ds(pl.multiple_of(c * chunk, chunk), chunk)

    def fetches(c):
        return (
            pltpu.make_async_copy(table_hbm.at[at(c)], table_ref.at[at(c)], sems.at[0, c]),
            pltpu.make_async_copy(mask_hbm.at[at(c)], mask_ref.at[at(c)], sems.at[1, c]),
        )

    turned = pltpu.make_async_copy(table_t_hbm, table_t_ref, sems.at[2, 0])

    @pl.when(step == 0)
    def _():
        for c in range(chunks):
            for fetch in fetches(c):
                fetch.start()
        turned.start()

    label = label_ref[...]
    user_t = user_t_ref[...]
    user = user_t.astype(F32).T.astype(BF)
    iota = lax.broadcasted_iota(jnp.int32, (chunk, block), 0)

    def fold(v, op):
        return op(v.reshape(chunk // 8, 8, block), axis=0)

    def first(c, carry):
        @pl.when(step == 0)
        def _():
            for fetch in fetches(c):
                fetch.wait()

        peak, pos = carry
        s = jnp.dot(table_ref[at(c), :], user_t, preferred_element_type=F32)
        pos = pos + fold(jnp.where(iota == label - c * chunk, s, 0.0), jnp.sum)
        s = s + jnp.concatenate([mask_ref[at(c), :]] * (block // LANES), axis=1)
        logits[at(c), :] = s
        return jnp.maximum(peak, fold(s, jnp.max)), pos

    peak, pos = lax.fori_loop(
        0,
        chunks,
        first,
        (jnp.full((8, block), -jnp.inf, F32), jnp.zeros((8, block), F32)),
    )
    pos = jnp.sum(pos, axis=0, keepdims=True)
    peak = jnp.maximum(jnp.max(peak, axis=0, keepdims=True), pos)

    def second(c, total):
        p = jnp.exp(logits[at(c), :] - peak)
        logits[at(c), :] = p
        return total + fold(p, jnp.sum)

    total = lax.fori_loop(0, chunks, second, jnp.zeros((8, block), F32))
    pos_exp = jnp.exp(pos - peak)
    total = jnp.sum(total, axis=0, keepdims=True) + pos_exp
    loss_ref[...] = peak + jnp.log(total) - pos
    scale = inv_count / total
    d_pos = (pos_exp / total - 1.0) * inv_count

    @pl.when(step == 0)
    def _():
        turned.wait()

    def back(add, store):
        def third(c, d_user_t):
            d = logits[at(c), :] * scale
            d = jnp.where(iota == label - c * chunk, d + d_pos, d).astype(BF)
            term = jnp.dot(d, user, preferred_element_type=F32)
            if add:
                term = grad_sum[at(c), :] + term
            if store:
                grad_ref[at(c), :] = term.astype(BF)
            else:
                grad_sum[at(c), :] = term
            return d_user_t + jnp.dot(table_t_ref[:, at(c)], d, preferred_element_type=F32)

        d_user_t = lax.fori_loop(0, chunks, third, jnp.zeros((feat, block), F32))
        d_user_t_ref[...] = d_user_t.astype(BF)

    @pl.when(step == 0)
    def _():
        back(False, False)

    @pl.when((step > 0) & (step < last))
    def _():
        back(True, False)

    @pl.when(step == last)
    def _():
        back(True, True)


def softmax_call(mask, table, table_t, user, labels, block=512, chunk=2048):
    n, feat = user.shape
    rows = table.shape[0]
    across = lambda h: pl.BlockSpec((h, block), lambda i: (0, i))
    any_place = pl.BlockSpec(memory_space=pl.ANY)
    return pl.pallas_call(
        functools.partial(softmax_body, 1.0 / n, chunk),
        grid=(n // block,),
        in_specs=[any_place] * 3
        + [across(feat), across(1)],
        out_specs=[across(feat), whole_vmem(), across(1)],
        out_shape=[
            jax.ShapeDtypeStruct((feat, n), BF),
            jax.ShapeDtypeStruct((rows, feat), BF),
            jax.ShapeDtypeStruct((1, n), F32),
        ],
        scratch_shapes=[
            pltpu.VMEM((rows, block), F32),
            pltpu.VMEM((rows, feat), F32),
            pltpu.VMEM((rows, LANES), F32),
            pltpu.VMEM((rows, feat), BF),
            pltpu.VMEM((feat, rows), BF),
            pltpu.SemaphoreType.DMA((3, rows // chunk)),
        ],
        compiler_params=params(58),
        name="sampled_softmax",
    )(mask, table, table_t, user.T, labels.reshape(1, n))


def sampled_mask(negatives, rows):
    high = lax.broadcasted_iota(jnp.int32, (rows // LANES, negatives.shape[0]), 0)
    low = lax.broadcasted_iota(jnp.int32, (LANES, negatives.shape[0]), 0)
    high_hot = (high == negatives[None, :] // LANES).astype(BF)
    low_hot = (low == negatives[None, :] % LANES).astype(BF)
    sampled = right_product(high_hot, low_hot).reshape(rows, 1)
    return jnp.broadcast_to(jnp.where(sampled > 0.5, F32(0.0), F32(-1e30)), (rows, LANES))


def left_product(first_op, second_op):
    return lax.dot_general(
        first_op, second_op, (((0,), (0,)), ((), ())), preferred_element_type=F32
    )


def right_product(first_op, second_op):
    return lax.dot_general(
        first_op, second_op, (((1,), (1,)), ((), ())), preferred_element_type=F32
    )


def gelu_back(pre_value, d_act):
    unused, pull = jax.vjp(jax.nn.gelu, pre_value)
    return pull(d_act)[0]


def in_range_ids(ids, lengths, offset):
    slot = lax.broadcasted_iota(jnp.int32, ids.shape, 1)
    kept = jnp.where(slot < lengths[:, None], ids + offset, -1)
    return jnp.pad(kept, ((0, 0), (0, LANES // 2 - ids.shape[1])), constant_values=-1)


def local(
    hot_table,
    tail_table,
    word_table,
    out_table,
    w_first,
    b_first,
    w_second,
    b_second,
    w_third,
    b_third,
    dense_feats,
    hist_ids,
    hist_len,
    search_ids,
    search_len,
    requests,
    labels,
    negatives,
):
    feat = hot_table.shape[1]
    hot_rows = hot_table.shape[0]
    owners, per_owner = requests.shape
    slots = owners * per_owner
    examples_dev = hist_ids.shape[0]
    examples_all = examples_dev * lax.axis_size("group") * lax.axis_size("wide")
    shard_rows = tail_table.shape[0]
    hist_float = hist_len[:, None].astype(F32)
    search_float = search_len[:, None].astype(F32)

    asked = lax.all_to_all(requests, "wide", split_axis=0, concat_axis=0, tiled=True)
    looked = gather_call(asked, tail_table)
    returned = lax.all_to_all(
        looked.reshape(owners, per_owner, feat), "wide", split_axis=0, concat_axis=0, tiled=True
    ).reshape(slots, feat)

    asked, negatives, looked = lax.optimization_barrier((asked, negatives, looked))
    ids = jnp.concatenate(
        [
            in_range_ids(hist_ids, hist_len, 0),
            in_range_ids(search_ids, search_len, hot_rows + slots),
        ],
        axis=1,
    )
    out_table_t = out_table.T
    mask = sampled_mask(negatives, out_table.shape[0])
    unroll = 16
    plan = row_plan(asked.reshape(slots), shard_rows, unroll)
    ids, out_table_t, mask, plan, looked = lax.optimization_barrier(
        (ids, out_table_t, mask, plan, looked)
    )
    hot_counts, slot_counts, word_counts, hot_sum, word_sum = counts_call(
        ids, hot_table, word_table, slots
    )

    hist_mean = (hot_sum + jnp.dot(slot_counts.astype(BF), returned, preferred_element_type=F32)) / hist_float
    search_mean = word_sum / search_float
    inputs = jnp.concatenate([hist_mean, search_mean, dense_feats.astype(F32)], axis=1).astype(BF)
    pre_first = jnp.dot(inputs, w_first, preferred_element_type=F32) + b_first.astype(F32)
    act_first = jax.nn.gelu(pre_first).astype(BF)
    pre_second = jnp.dot(act_first, w_second, preferred_element_type=F32) + b_second.astype(F32)
    act_second = jax.nn.gelu(pre_second).astype(BF)
    user = (jnp.dot(act_second, w_third, preferred_element_type=F32) + b_third.astype(F32)).astype(
        BF
    )

    d_user_t, out_grad, per_example = softmax_call(mask, out_table, out_table_t, user, labels)
    d_user = d_user_t.T
    d_pre_second = gelu_back(pre_second, right_product(d_user, w_third)).astype(BF)
    d_pre_first = gelu_back(pre_first, right_product(d_pre_second, w_second)).astype(BF)
    d_inputs = right_product(d_pre_first, w_first[: 2 * feat])

    hot_grad, word_grad = spread_call(
        (hot_counts, word_counts), (hist_float, search_float), d_inputs, (0, feat), feat, 4
    )
    w1_grad = left_product(inputs, d_pre_first).astype(BF)
    w2_grad = left_product(act_first, d_pre_second).astype(BF)
    w3_grad = left_product(act_second, d_user).astype(BF)
    small = [
        per_example,
        jnp.sum(d_pre_first.astype(F32), axis=0),
        jnp.sum(d_pre_second.astype(F32), axis=0),
        jnp.sum(d_user.astype(F32), axis=0),
    ]
    small_rows = jnp.concatenate([x.reshape(-1, feat) for x in small], axis=0).astype(BF)
    w3_rows = w3_grad.shape[0]
    small_rows = jnp.pad(small_rows, ((0, -small_rows.shape[0] % 16), (0, 0)))
    packed = (
        hot_grad,
        word_grad,
        out_grad,
        w1_grad,
        w2_grad,
        jnp.concatenate([w3_grad, small_rows], axis=0),
    )
    packed, slot_counts = lax.optimization_barrier((packed, slot_counts))
    summed = lax.psum(packed, ("group", "wide"))

    (slot_grad,) = spread_call((slot_counts,), (hist_float,), d_inputs, (0,), feat, 4)
    owed = lax.all_to_all(
        slot_grad.reshape(owners, per_owner, feat), "wide", split_axis=0, concat_axis=0, tiled=True
    ).reshape(slots, feat)
    own = add_rows_call(plan, owed, shard_rows, unroll, 4)
    others = [lax.ppermute(x, "group", [(0, 1), (1, 0)]) for x in own]
    tail_grad = add_pair_call(own, others)
    summed, tail_grad = lax.optimization_barrier((summed, tail_grad))
    hot_all, word_all, out_all, w2_all, w1_all, w3_all, losses, b1_all, b2_all, b3_all = widen_call(
        (summed[0], summed[1], summed[2], summed[4]),
        summed[3],
        summed[5],
        w3_rows,
        examples_dev // feat,
        (b_first.shape[0], b_second.shape[0], b_third.shape[0]),
        4,
    )
    loss_value = jnp.sum(losses) / examples_all
    return (
        loss_value,
        hot_all,
        tail_grad,
        word_all,
        out_all,
        w1_all,
        b1_all[0],
        w2_all,
        b2_all[0],
        w3_all,
        b3_all[0],
    )


def solution(mesh):
    split = ("group", "wide")
    in_specs = (
        (P(), P("wide", None))
        + (P(),) * 8
        + (P(split, None), P(split, None), P(split), P(split, None), P(split), P(split, None))
        + (P(split), P())
    )
    out_specs = (P(), P(), P("wide", None)) + (P(),) * 8
    return jax.shard_map(local, mesh=mesh, in_specs=in_specs, out_specs=out_specs, check_vma=False)
```

```python
import functools

import jax
import jax.numpy as jnp
from jax import lax
from jax.experimental import pallas as pl
from jax.experimental.pallas import tpu as pltpu
from jax.sharding import PartitionSpec as P

BF = jnp.bfloat16
F32 = jnp.float32
LANES = 128
MIB = 1024 * 1024


def params(mib):
    return pltpu.CompilerParams(vmem_limit_bytes=mib * MIB)


def whole_vmem():
    return pl.BlockSpec(memory_space=pltpu.VMEM)


def whole_smem():
    return pl.BlockSpec(memory_space=pltpu.SMEM)


def counts_body(cuts, ids_ref, hot_ref, word_ref, *refs):
    count_refs = refs[: len(cuts)]
    hist_ref, word_sum_ref, scratch, low_ref, high_ref = refs[len(cuts) :]
    block = ids_ref.shape[0]
    groups = sum(cuts)
    rows = groups + 8
    ids = ids_ref[...]
    low_ref[...] = (ids & (LANES - 1)).astype(F32)
    place = lax.broadcasted_iota(jnp.int32, ids.shape, 0) & 7
    high_ref[...] = (jnp.where(ids < 0, -64, ids >> 7) + place).astype(F32)
    low_iota = lax.broadcasted_iota(jnp.int32, (LANES, LANES), 0).astype(BF)
    high_iota = lax.broadcasted_iota(jnp.int32, (rows, LANES), 0).astype(BF)
    one = jnp.ones((), BF)
    zero = jnp.zeros((), BF)
    unroll = block

    def build(i, carry):
        for k in range(unroll):
            e = i * unroll + k
            low = jnp.broadcast_to(low_ref[pl.ds(e, 1), :], (LANES, LANES)).astype(BF)
            high = jnp.broadcast_to(high_ref[pl.ds(e, 1), :], (rows, LANES)).astype(BF)
            low_hot = jnp.where(low_iota == low, one, zero)
            high_hot = jnp.where(high_iota == high, one, zero)
            scratch[pl.ds(pl.multiple_of(e * rows, 8), rows), :] = right_product(high_hot, low_hot)
        return carry

    lax.fori_loop(0, block // unroll, build, 0)

    def regroup(i, carry):
        here = pl.ds(pl.multiple_of(i * 32, 32), 32)
        g = 0
        for ref, cut in zip(count_refs, cuts):
            for c in range(cut):
                eights = [
                    scratch[pl.ds((i * 32 + e) * rows + g, 8, stride=rows + 1), :]
                    for e in range(0, 32, 8)
                ]
                ref[here, c * LANES : (c + 1) * LANES] = jnp.concatenate(eights, axis=0).astype(
                    jnp.int8
                )
                g += 1
        return carry

    lax.fori_loop(0, block // 32, regroup, 0)
    hist_ref[...] = jnp.dot(count_refs[0][...].astype(BF), hot_ref[...], preferred_element_type=F32)
    word_sum_ref[...] = jnp.dot(
        count_refs[-1][...].astype(BF), word_ref[...], preferred_element_type=F32
    )


def counts_call(ids, hot, word, tail_rows, block=128):
    n = ids.shape[0]
    feat = hot.shape[1]
    widths = (hot.shape[0], tail_rows, word.shape[0])
    cuts = tuple(w // LANES for w in widths)
    rows_of = lambda w: pl.BlockSpec((block, w), lambda i: (i, 0))
    fixed = lambda s: pl.BlockSpec(s, lambda i: (0, 0))
    return pl.pallas_call(
        functools.partial(counts_body, cuts),
        grid=(n // block,),
        in_specs=[rows_of(LANES), fixed(hot.shape), fixed(word.shape)],
        out_specs=[rows_of(w) for w in widths] + [rows_of(feat)] * 2,
        out_shape=[jax.ShapeDtypeStruct((n, w), jnp.int8) for w in widths]
        + [jax.ShapeDtypeStruct((n, feat), F32)] * 2,
        scratch_shapes=[pltpu.VMEM((block * (sum(cuts) + 8), LANES), F32)]
        + [pltpu.VMEM((block, LANES), F32)] * 2,
        compiler_params=params(56),
        name="counts",
    )(ids, hot, word)


def gather_body(parts, ids_ref, table_hbm, out_hbm, table, wide, picked, out, sems):
    rows = table.shape[0]
    owners, each = ids_ref.shape
    here = lambda i, size: pl.ds(pl.multiple_of(i * size, size), size)
    given = rows // parts
    taken = owners // parts
    inward = [
        pltpu.make_async_copy(
            table_hbm.at[here(p, given)], table.at[here(p, given)], sems.at[0, p]
        )
        for p in range(parts)
    ]
    outward = [
        pltpu.make_async_copy(
            out.at[here(p, taken * each)], out_hbm.at[here(p, taken * each)], sems.at[1, p]
        )
        for p in range(parts)
    ]
    for copy in inward:
        copy.start()
    wide[:8, :] = jnp.zeros((8, LANES), F32)
    for p in range(parts):
        inward[p].wait()

        def widen(i, carry, p=p):
            i = i + p * (given // 128)
            t = table[here(i, 128), :].astype(F32)
            wide[pl.ds(8 + i * 256, 128, stride=2), :] = t[:, :LANES]
            wide[pl.ds(9 + i * 256, 128, stride=2), :] = t[:, LANES:]
            return carry

        lax.fori_loop(0, given // 128, widen, 0)

    for p in range(parts):

        def pick(owner, carry):
            for k in range(each):
                at = owner * each + k
                picked[pl.ds(at * 2, 2), :] = wide[pl.ds(ids_ref[owner, k] * 2 + 8, 2), :]
            return carry

        lax.fori_loop(p * taken, (p + 1) * taken, pick, 0)

        def join(i, carry):
            left = picked[pl.ds(i * 256, 128, stride=2), :]
            right = picked[pl.ds(i * 256 + 1, 128, stride=2), :]
            out[here(i, 128), :] = jnp.concatenate([left, right], axis=1).astype(BF)
            return carry

        lax.fori_loop(p * taken * each // 128, (p + 1) * taken * each // 128, join, 0)
        outward[p].start()
    for copy in outward:
        copy.wait()


def gather_call(ids, table, parts=8):
    rows, feat = table.shape
    count = ids.size
    return pl.pallas_call(
        functools.partial(gather_body, parts),
        in_specs=[whole_smem(), pl.BlockSpec(memory_space=pl.ANY)],
        out_specs=pl.BlockSpec(memory_space=pl.ANY),
        out_shape=jax.ShapeDtypeStruct((count, feat), BF),
        scratch_shapes=[
            pltpu.VMEM((rows, feat), BF),
            pltpu.VMEM((2 * rows + 8, LANES), F32),
            pltpu.VMEM((2 * count, LANES), F32),
            pltpu.VMEM((count, feat), BF),
            pltpu.SemaphoreType.DMA((2, parts)),
        ],
        compiler_params=params(60),
        name="gather_rows",
    )(ids, table)


def add_rows_body(unroll, given_parts, ids_ref, again_ref, clash_ref, *refs):
    given_refs, out_refs = refs[:given_parts], refs[given_parts:-3]
    total_a, total_b, wide = refs[-3:]
    count = sum(ref.shape[0] for ref in given_refs)
    part = out_refs[0].shape[0]
    rows = part * len(out_refs)

    def clear(i, carry):
        for total in (total_a, total_b):
            total[pl.ds(pl.multiple_of(i * 256, 256), 256), :] = jnp.zeros((256, LANES), F32)
        return carry

    lax.fori_loop(0, rows // 128, clear, 0)

    start = 0
    for ref in given_refs:

        def widen(i, carry, ref=ref, start=start):
            t = ref[pl.ds(pl.multiple_of(i * 128, 128), 128), :].astype(F32)
            wide[pl.ds(2 * start + i * 256, 128, stride=2), :] = t[:, :LANES]
            wide[pl.ds(2 * start + i * 256 + 1, 128, stride=2), :] = t[:, LANES:]
            return carry

        lax.fori_loop(0, ref.shape[0] // 128, widen, 0)
        start += ref.shape[0]

    def given(at):
        return wide[pl.ds(at * 2, 2), :]

    def add(i, carry):
        for total, base in ((total_a, i * 2 * unroll), (total_b, (i * 2 + 1) * unroll)):
            places = [pl.ds(ids_ref[base + k] * 2, 2) for k in range(unroll)]
            sums = [total[p, :] + given(base + k) for k, p in enumerate(places)]
            for p, v in zip(places, sums):
                total[p, :] = v
        return carry

    lax.fori_loop(0, count // (2 * unroll), add, 0)

    groups = count // unroll
    section = 16

    def check(i, carry):
        @pl.when(clash_ref[groups + i] != 0)
        def _():
            def add_again(j, inner):
                group = i * section + j

                @pl.when(clash_ref[group] != 0)
                def _():
                    for k in range(unroll):
                        p = pl.ds(again_ref[group * unroll + k] * 2, 2)
                        total_a[p, :] = total_a[p, :] + given(group * unroll + k)

                return inner

            lax.fori_loop(0, section, add_again, 0)

        return carry

    lax.fori_loop(0, groups // section, check, 0)

    for n, out_ref in enumerate(out_refs):

        def join(i, carry, n=n, out_ref=out_ref):
            left = pl.ds(n * part * 2 + i * 256, 128, stride=2)
            right = pl.ds(n * part * 2 + i * 256 + 1, 128, stride=2)
            both = [total_a[p, :] + total_b[p, :] for p in (left, right)]
            here = pl.ds(pl.multiple_of(i * 128, 128), 128)
            out_ref[here, :] = jnp.concatenate(both, axis=1).astype(out_ref.dtype)
            return carry

        lax.fori_loop(0, part // 128, join, 0)


def row_plan(ids, rows, unroll):
    grouped = ids.reshape(-1, unroll)
    spare = rows + lax.broadcasted_iota(jnp.int32, grouped.shape, 1)
    earlier = lax.broadcasted_iota(jnp.int32, (unroll, unroll), 1) < lax.broadcasted_iota(
        jnp.int32, (unroll, unroll), 0
    )
    same = (grouped[:, :, None] == grouped[:, None, :]) & earlier[None]
    twice = jnp.any(same, axis=2) & (grouped >= 0)
    once = jnp.where((grouped >= 0) & ~twice, grouped, spare)
    again = jnp.where(twice, grouped, spare)
    clash = jnp.any(twice, axis=1).astype(jnp.int32)
    sections = jnp.max(clash.reshape(-1, 16), axis=1)
    return once.reshape(-1), again.reshape(-1), jnp.concatenate([clash, sections])


def add_rows_call(plan, given, rows, unroll, parts):
    count, feat = sum(x.shape[0] for x in given), given[0].shape[1]
    return pl.pallas_call(
        functools.partial(add_rows_body, unroll, len(given)),
        in_specs=[whole_smem()] * 3 + [whole_vmem()] * len(given),
        out_specs=[whole_vmem()] * parts,
        out_shape=[jax.ShapeDtypeStruct((rows // parts, feat), BF)] * parts,
        scratch_shapes=[pltpu.VMEM((2 * (rows + unroll), LANES), F32)] * 2
        + [pltpu.VMEM((2 * count, LANES), F32)],
        compiler_params=params(48),
        name="add_rows",
        cost_estimate=pl.CostEstimate(flops=0, bytes_accessed=0, transcendentals=0),
    )(*plan, *given)


def spread_body(pairs, firsts, d_inputs_ref, *refs):
    part_refs = refs[3 * pairs :]
    feat = part_refs[0].shape[1]

    @pl.when(pl.program_id(0) == 0)
    def _():
        for i, first in enumerate(firsts):
            d_mean = d_inputs_ref[:, first : first + feat]
            part_refs[i][...] = (d_mean / refs[2 * i + 1][...]).astype(BF)

    for i in range(pairs):
        counts_ref, out_ref = refs[2 * i], refs[2 * pairs + i]
        out_ref[...] = left_product(counts_ref[...].astype(BF), part_refs[i][...]).astype(BF)


def spread_call(counts, lengths, d_inputs, firsts, feat, steps):
    n = d_inputs.shape[0]
    specs, args = [whole_vmem()], [d_inputs]
    for c, x in zip(counts, lengths):
        specs += [pl.BlockSpec((n, c.shape[1] // steps), lambda i: (0, i)), whole_vmem()]
        args += [c, x]
    return pl.pallas_call(
        functools.partial(spread_body, len(counts), firsts),
        grid=(steps,),
        in_specs=specs,
        out_specs=[pl.BlockSpec((c.shape[1] // steps, feat), lambda i: (i, 0)) for c in counts],
        out_shape=[jax.ShapeDtypeStruct((c.shape[1], feat), BF) for c in counts],
        scratch_shapes=[pltpu.VMEM((n, feat), BF)] * len(counts),
        compiler_params=params(60),
        name="spread",
    )(*args)


def slot_spread_body(cuts, counts_ref, length_ref, d_inputs_ref, *refs):
    out_refs, part_ref = refs[:-1], refs[-1]
    feat = part_ref.shape[1]

    @pl.when(pl.program_id(0) == 0)
    def _():
        part_ref[...] = (d_inputs_ref[:, :feat] / length_ref[...]).astype(BF)

    grad = left_product(counts_ref[...].astype(BF), part_ref[...])
    grad = grad.reshape(-1, sum(cuts), feat)
    start = 0
    for ref, cut in zip(out_refs, cuts):
        ref[...] = grad[:, start : start + cut, :].astype(BF)
        start += cut


def slot_spread_call(counts, lengths, d_inputs, feat, cuts, steps):
    n, slots = counts.shape
    owners = slots // sum(cuts)
    return pl.pallas_call(
        functools.partial(slot_spread_body, cuts),
        grid=(steps,),
        in_specs=[pl.BlockSpec((n, slots // steps), lambda i: (0, i)), whole_vmem(), whole_vmem()],
        out_specs=[pl.BlockSpec((owners // steps, cut, feat), lambda i: (i, 0, 0)) for cut in cuts],
        out_shape=[jax.ShapeDtypeStruct((owners, cut, feat), BF) for cut in cuts],
        scratch_shapes=[pltpu.VMEM((n, feat), BF)],
        compiler_params=params(60),
        cost_estimate=pl.CostEstimate(flops=0, bytes_accessed=0, transcendentals=0),
        name="slot_spread",
    )(counts, lengths, d_inputs)


def widen_body(blocked, *refs):
    given, outs = refs[: blocked + 2], refs[blocked + 2 :]
    for x_ref, out_ref in zip(given[:blocked], outs[:blocked]):
        out_ref[...] = x_ref[...].astype(F32)
    first_ref, last_ref = given[blocked:]
    first_out_ref, last_out_ref, loss_ref, *bias_refs = outs[blocked:]

    @pl.when(pl.program_id(0) == 0)
    def _():
        rows, feat = last_out_ref.shape
        first_out_ref[...] = first_ref[...].astype(F32)
        last_out_ref[...] = last_ref[:rows, :].astype(F32)
        small = last_ref[rows:, :].astype(F32)
        start = loss_ref.shape[0]
        loss_ref[...] = small[:start]
        for ref in bias_refs:
            for i in range(ref.shape[1] // feat):
                ref[:, i * feat : (i + 1) * feat] = small[start : start + 1]
                start += 1


def widen_call(arrays, first, last, last_rows, loss_rows, widths, steps):
    feat = last.shape[1]
    spec = lambda a: pl.BlockSpec((a.shape[0] // steps, a.shape[1]), lambda i: (i, 0))
    shapes = [a.shape for a in (*arrays, first)] + [(last_rows, feat), (loss_rows, feat)]
    shapes += [(1, w) for w in widths]
    return pl.pallas_call(
        functools.partial(widen_body, len(arrays)),
        grid=(steps,),
        in_specs=[spec(a) for a in arrays] + [whole_vmem()] * 2,
        out_specs=[spec(a) for a in arrays] + [whole_vmem()] * (len(shapes) - len(arrays)),
        out_shape=[jax.ShapeDtypeStruct(s, F32) for s in shapes],
        compiler_params=params(60),
        name="widen",
    )(*arrays, first, last)


def add_parts_body(*refs):
    count = len(refs) // 2
    for k in range(count):

        @pl.when(pl.program_id(0) == k)
        def _(k=k):
            refs[-1][...] = refs[k][...].astype(F32) + refs[count + k][...].astype(F32)


def add_pair_call(own, others):
    rows, feat = own[0].shape
    spec = pl.BlockSpec((rows, feat), lambda i: (0, 0))
    return pl.pallas_call(
        add_parts_body,
        grid=(len(own),),
        in_specs=[spec] * (2 * len(own)),
        out_specs=pl.BlockSpec((rows, feat), lambda i: (i, 0)),
        out_shape=jax.ShapeDtypeStruct((rows * len(own), feat), F32),
        compiler_params=params(60),
        cost_estimate=pl.CostEstimate(flops=0, bytes_accessed=0, transcendentals=0),
        name="add_parts",
    )(*own, *others)


def softmax_body(
    inv_count,
    chunk,
    mask_hbm,
    table_hbm,
    table_t_hbm,
    user_t_ref,
    label_ref,
    d_user_t_ref,
    grad_ref,
    loss_ref,
    logits,
    grad_sum,
    mask_ref,
    table_ref,
    table_t_ref,
    sems,
):
    rows, feat = table_ref.shape
    block = user_t_ref.shape[1]
    chunks = rows // chunk
    step = pl.program_id(0)
    last = pl.num_programs(0) - 1

    def at(c):
        return pl.ds(pl.multiple_of(c * chunk, chunk), chunk)

    def fetches(c):
        return (
            pltpu.make_async_copy(table_hbm.at[at(c)], table_ref.at[at(c)], sems.at[0, c]),
            pltpu.make_async_copy(mask_hbm.at[at(c)], mask_ref.at[at(c)], sems.at[1, c]),
        )

    turned = pltpu.make_async_copy(table_t_hbm, table_t_ref, sems.at[2, 0])

    @pl.when(step == 0)
    def _():
        for c in range(chunks):
            for fetch in fetches(c):
                fetch.start()
        turned.start()

    label = label_ref[...]
    user_t = user_t_ref[...]
    user = user_t.astype(F32).T.astype(BF)
    sublane = lax.broadcasted_iota(jnp.int32, (8, block), 0)

    def hits(c):
        place = label - c * chunk - sublane
        return jnp.concatenate([place == 8 * g for g in range(chunk // 8)], axis=0)


    def fold(v, op):
        return op(v.reshape(chunk // 8, 8, block), axis=0)

    def first(c, carry):
        @pl.when(step == 0)
        def _():
            for fetch in fetches(c):
                fetch.wait()

        peak, pos = carry
        s = jnp.dot(table_ref[at(c), :], user_t, preferred_element_type=F32)
        pos = pos + fold(jnp.where(hits(c), s, 0.0), jnp.sum)
        s = s + jnp.concatenate([mask_ref[at(c), :]] * (block // LANES), axis=1)
        logits[at(c), :] = s
        return jnp.maximum(peak, fold(s, jnp.max)), pos

    peak, pos = lax.fori_loop(
        0,
        chunks,
        first,
        (jnp.full((8, block), -jnp.inf, F32), jnp.zeros((8, block), F32)),
    )
    pos = jnp.sum(pos, axis=0, keepdims=True)
    peak = jnp.maximum(jnp.max(peak, axis=0, keepdims=True), pos)

    def second(c, total):
        p = jnp.exp(logits[at(c), :] - peak)
        logits[at(c), :] = p
        return total + fold(p, jnp.sum)

    total = lax.fori_loop(0, chunks, second, jnp.zeros((8, block), F32))
    pos_exp = jnp.exp(pos - peak)
    total = jnp.sum(total, axis=0, keepdims=True) + pos_exp
    loss_ref[...] = peak + jnp.log(total) - pos
    scale = inv_count / total
    d_pos = (pos_exp / total - 1.0) * inv_count

    @pl.when(step == 0)
    def _():
        turned.wait()

    def back(add, store):
        def third(c, d_user_t):
            d = logits[at(c), :] * scale
            d = jnp.where(hits(c), d + d_pos, d).astype(BF)
            term = jnp.dot(d, user, preferred_element_type=F32)
            if add:
                term = grad_sum[at(c), :] + term
            if store:
                grad_ref[at(c), :] = term.astype(BF)
            else:
                grad_sum[at(c), :] = term
            return d_user_t + jnp.dot(table_t_ref[:, at(c)], d, preferred_element_type=F32)

        d_user_t = lax.fori_loop(0, chunks, third, jnp.zeros((feat, block), F32))
        d_user_t_ref[...] = d_user_t.astype(BF)

    @pl.when(step == 0)
    def _():
        back(False, False)

    @pl.when((step > 0) & (step < last))
    def _():
        back(True, False)

    @pl.when(step == last)
    def _():
        back(True, True)


def softmax_call(mask, table, table_t, user, labels, block=512, chunk=4096):
    n, feat = user.shape
    rows = table.shape[0]
    across = lambda h: pl.BlockSpec((h, block), lambda i: (0, i))
    any_place = pl.BlockSpec(memory_space=pl.ANY)
    return pl.pallas_call(
        functools.partial(softmax_body, 1.0 / n, chunk),
        grid=(n // block,),
        in_specs=[any_place] * 3
        + [across(feat), across(1)],
        out_specs=[across(feat), whole_vmem(), across(1)],
        out_shape=[
            jax.ShapeDtypeStruct((feat, n), BF),
            jax.ShapeDtypeStruct((rows, feat), BF),
            jax.ShapeDtypeStruct((1, n), F32),
        ],
        scratch_shapes=[
            pltpu.VMEM((rows, block), F32),
            pltpu.VMEM((rows, feat), F32),
            pltpu.VMEM((rows, LANES), F32),
            pltpu.VMEM((rows, feat), BF),
            pltpu.VMEM((feat, rows), BF),
            pltpu.SemaphoreType.DMA((3, rows // chunk)),
        ],
        compiler_params=params(58),
        name="sampled_softmax",
    )(mask, table, table_t, user.T, labels.reshape(1, n))


def sampled_mask(negatives, rows):
    high = lax.broadcasted_iota(jnp.int32, (rows // LANES, negatives.shape[0]), 0)
    low = lax.broadcasted_iota(jnp.int32, (LANES, negatives.shape[0]), 0)
    high_hot = (high == negatives[None, :] // LANES).astype(BF)
    low_hot = (low == negatives[None, :] % LANES).astype(BF)
    sampled = right_product(high_hot, low_hot).reshape(rows, 1)
    return jnp.broadcast_to(jnp.where(sampled > 0.5, F32(0.0), F32(-1e30)), (rows, LANES))


def left_product(first_op, second_op):
    return lax.dot_general(
        first_op, second_op, (((0,), (0,)), ((), ())), preferred_element_type=F32
    )


def right_product(first_op, second_op):
    return lax.dot_general(
        first_op, second_op, (((1,), (1,)), ((), ())), preferred_element_type=F32
    )


def gelu_back(pre_value, d_act):
    unused, pull = jax.vjp(jax.nn.gelu, pre_value)
    return pull(d_act)[0]


def in_range_ids(ids, lengths, offset):
    slot = lax.broadcasted_iota(jnp.int32, ids.shape, 1)
    kept = jnp.where(slot < lengths[:, None], ids + offset, -1)
    return jnp.pad(kept, ((0, 0), (0, LANES // 2 - ids.shape[1])), constant_values=-1)


def local(
    hot_table,
    tail_table,
    word_table,
    out_table,
    w_first,
    b_first,
    w_second,
    b_second,
    w_third,
    b_third,
    dense_feats,
    hist_ids,
    hist_len,
    search_ids,
    search_len,
    requests,
    labels,
    negatives,
):
    feat = hot_table.shape[1]
    hot_rows = hot_table.shape[0]
    owners, per_owner = requests.shape
    slots = owners * per_owner
    examples_dev = hist_ids.shape[0]
    examples_all = examples_dev * lax.axis_size("group") * lax.axis_size("wide")
    shard_rows = tail_table.shape[0]
    hist_float = hist_len[:, None].astype(F32)
    search_float = search_len[:, None].astype(F32)

    asked = lax.all_to_all(requests, "wide", split_axis=0, concat_axis=0, tiled=True)
    looked = gather_call(asked, tail_table)
    returned = lax.all_to_all(
        looked.reshape(owners, per_owner, feat), "wide", split_axis=0, concat_axis=0, tiled=True
    ).reshape(slots, feat)

    asked, negatives, looked = lax.optimization_barrier((asked, negatives, looked))
    ids = jnp.concatenate(
        [
            in_range_ids(hist_ids, hist_len, 0),
            in_range_ids(search_ids, search_len, hot_rows + slots),
        ],
        axis=1,
    )
    out_table_t = out_table.T
    mask = sampled_mask(negatives, out_table.shape[0])
    unroll = 16
    cuts = (16, 16, 16, 32, 16, 16, 16)
    edges = [sum(cuts[:i]) for i in range(len(cuts) + 1)]
    asked_parts = [asked[:, i:j].reshape(-1) for i, j in zip(edges, edges[1:])]
    plan = row_plan(jnp.concatenate(asked_parts), shard_rows, unroll)
    ids, out_table_t, mask, plan, looked = lax.optimization_barrier(
        (ids, out_table_t, mask, plan, looked)
    )
    hot_counts, slot_counts, word_counts, hot_sum, word_sum = counts_call(
        ids, hot_table, word_table, slots
    )

    hist_mean = (hot_sum + jnp.dot(slot_counts.astype(BF), returned, preferred_element_type=F32)) / hist_float
    search_mean = word_sum / search_float
    inputs = jnp.concatenate([hist_mean, search_mean, dense_feats.astype(F32)], axis=1).astype(BF)
    pre_first = jnp.dot(inputs, w_first, preferred_element_type=F32) + b_first.astype(F32)
    act_first = jax.nn.gelu(pre_first).astype(BF)
    pre_second = jnp.dot(act_first, w_second, preferred_element_type=F32) + b_second.astype(F32)
    act_second = jax.nn.gelu(pre_second).astype(BF)
    user = (jnp.dot(act_second, w_third, preferred_element_type=F32) + b_third.astype(F32)).astype(
        BF
    )

    d_user_t, out_grad, per_example = softmax_call(mask, out_table, out_table_t, user, labels)
    d_user = d_user_t.T
    d_pre_second = gelu_back(pre_second, right_product(d_user, w_third)).astype(BF)
    d_pre_first = gelu_back(pre_first, right_product(d_pre_second, w_second)).astype(BF)
    d_inputs = right_product(d_pre_first, w_first[: 2 * feat])

    hot_grad, word_grad = spread_call(
        (hot_counts, word_counts), (hist_float, search_float), d_inputs, (0, feat), feat, 4
    )
    w1_grad = left_product(inputs, d_pre_first).astype(BF)
    w2_grad = left_product(act_first, d_pre_second).astype(BF)
    w3_grad = left_product(act_second, d_user).astype(BF)
    small = [
        per_example,
        jnp.sum(d_pre_first.astype(F32), axis=0),
        jnp.sum(d_pre_second.astype(F32), axis=0),
        jnp.sum(d_user.astype(F32), axis=0),
    ]
    small_rows = jnp.concatenate([x.reshape(-1, feat) for x in small], axis=0).astype(BF)
    w3_rows = w3_grad.shape[0]
    small_rows = jnp.pad(small_rows, ((0, -small_rows.shape[0] % 16), (0, 0)))
    packed = (
        hot_grad,
        word_grad,
        out_grad,
        w1_grad,
        w2_grad,
        jnp.concatenate([w3_grad, small_rows], axis=0),
    )
    packed, slot_counts = lax.optimization_barrier((packed, slot_counts))
    summed = lax.psum(packed, ("group", "wide"))

    slot_grads = slot_spread_call(slot_counts, hist_float, d_inputs, feat, cuts, 4)
    owed = []
    for part in slot_grads:
        if owed:
            part, owed[-1] = lax.optimization_barrier((part, owed[-1]))
        owed.append(lax.all_to_all(part, "wide", split_axis=0, concat_axis=0, tiled=True))
    owed = [x.reshape(-1, feat) for x in owed]
    own = add_rows_call(plan, owed, shard_rows, unroll, 4)
    others = [lax.ppermute(x, "group", [(0, 1), (1, 0)]) for x in own]
    tail_grad = add_pair_call(own, others)
    summed, tail_grad = lax.optimization_barrier((summed, tail_grad))
    hot_all, word_all, out_all, w2_all, w1_all, w3_all, losses, b1_all, b2_all, b3_all = widen_call(
        (summed[0], summed[1], summed[2], summed[4]),
        summed[3],
        summed[5],
        w3_rows,
        examples_dev // feat,
        (b_first.shape[0], b_second.shape[0], b_third.shape[0]),
        4,
    )
    loss_value = jnp.sum(losses) / examples_all
    return (
        loss_value,
        hot_all,
        tail_grad,
        word_all,
        out_all,
        w1_all,
        b1_all[0],
        w2_all,
        b2_all[0],
        w3_all,
        b3_all[0],
    )


def solution(mesh):
    split = ("group", "wide")
    in_specs = (
        (P(), P("wide", None))
        + (P(),) * 8
        + (P(split, None), P(split, None), P(split), P(split, None), P(split), P(split, None))
        + (P(split), P())
    )
    out_specs = (P(), P(), P("wide", None)) + (P(),) * 8
    return jax.shard_map(local, mesh=mesh, in_specs=in_specs, out_specs=out_specs, check_vma=False)
```

```python
import functools

import jax
import jax.numpy as jnp
from jax import lax
from jax.experimental import pallas as pl
from jax.experimental.pallas import tpu as pltpu
from jax.sharding import PartitionSpec as P

BF = jnp.bfloat16
F32 = jnp.float32
LANES = 128
MIB = 1024 * 1024


def params(mib):
    return pltpu.CompilerParams(vmem_limit_bytes=mib * MIB)


def whole_vmem():
    return pl.BlockSpec(memory_space=pltpu.VMEM)


def whole_smem():
    return pl.BlockSpec(memory_space=pltpu.SMEM)


def counts_body(cuts, ids_ref, hot_ref, word_ref, *refs):
    count_refs = refs[: len(cuts)]
    hist_ref, word_sum_ref, scratch, low_ref, high_ref = refs[len(cuts) :]
    block = ids_ref.shape[0]
    groups = sum(cuts)
    rows = groups + 8
    ids = ids_ref[...]
    low_ref[...] = (ids & (LANES - 1)).astype(F32)
    place = lax.broadcasted_iota(jnp.int32, ids.shape, 0) & 7
    high_ref[...] = (jnp.where(ids < 0, -64, ids >> 7) + place).astype(F32)
    low_iota = lax.broadcasted_iota(jnp.int32, (LANES, LANES), 0).astype(BF)
    high_iota = lax.broadcasted_iota(jnp.int32, (rows, LANES), 0).astype(BF)
    one = jnp.ones((), BF)
    zero = jnp.zeros((), BF)
    unroll = block

    def build(i, carry):
        for k in range(unroll):
            e = i * unroll + k
            low = jnp.broadcast_to(low_ref[pl.ds(e, 1), :], (LANES, LANES)).astype(BF)
            high = jnp.broadcast_to(high_ref[pl.ds(e, 1), :], (rows, LANES)).astype(BF)
            low_hot = jnp.where(low_iota == low, one, zero)
            high_hot = jnp.where(high_iota == high, one, zero)
            scratch[pl.ds(pl.multiple_of(e * rows, 8), rows), :] = right_product(high_hot, low_hot)
        return carry

    lax.fori_loop(0, block // unroll, build, 0)

    def regroup(i, carry):
        here = pl.ds(pl.multiple_of(i * 32, 32), 32)
        g = 0
        for ref, cut in zip(count_refs, cuts):
            for c in range(cut):
                eights = [
                    scratch[pl.ds((i * 32 + e) * rows + g, 8, stride=rows + 1), :]
                    for e in range(0, 32, 8)
                ]
                ref[here, c * LANES : (c + 1) * LANES] = jnp.concatenate(eights, axis=0).astype(
                    jnp.int8
                )
                g += 1
        return carry

    lax.fori_loop(0, block // 32, regroup, 0)
    hist_ref[...] = jnp.dot(count_refs[0][...].astype(BF), hot_ref[...], preferred_element_type=F32)
    word_sum_ref[...] = jnp.dot(
        count_refs[-1][...].astype(BF), word_ref[...], preferred_element_type=F32
    )


def counts_call(ids, hot, word, tail_rows, block=128):
    n = ids.shape[0]
    feat = hot.shape[1]
    widths = (hot.shape[0], tail_rows, word.shape[0])
    cuts = tuple(w // LANES for w in widths)
    rows_of = lambda w: pl.BlockSpec((block, w), lambda i: (i, 0))
    fixed = lambda s: pl.BlockSpec(s, lambda i: (0, 0))
    return pl.pallas_call(
        functools.partial(counts_body, cuts),
        grid=(n // block,),
        in_specs=[rows_of(LANES), fixed(hot.shape), fixed(word.shape)],
        out_specs=[rows_of(w) for w in widths] + [rows_of(feat)] * 2,
        out_shape=[jax.ShapeDtypeStruct((n, w), jnp.int8) for w in widths]
        + [jax.ShapeDtypeStruct((n, feat), F32)] * 2,
        scratch_shapes=[pltpu.VMEM((block * (sum(cuts) + 8), LANES), F32)]
        + [pltpu.VMEM((block, LANES), F32)] * 2,
        compiler_params=params(56),
        name="counts",
    )(ids, hot, word)


def gather_body(parts, ids_ref, table_hbm, out_hbm, table, wide, picked, out, sems):
    rows = table.shape[0]
    owners, each = ids_ref.shape
    here = lambda i, size: pl.ds(pl.multiple_of(i * size, size), size)
    given = rows // parts
    taken = owners // parts
    inward = [
        pltpu.make_async_copy(
            table_hbm.at[here(p, given)], table.at[here(p, given)], sems.at[0, p]
        )
        for p in range(parts)
    ]
    outward = [
        pltpu.make_async_copy(
            out.at[here(p, taken * each)], out_hbm.at[here(p, taken * each)], sems.at[1, p]
        )
        for p in range(parts)
    ]
    for copy in inward:
        copy.start()
    wide[:8, :] = jnp.zeros((8, LANES), F32)
    for p in range(parts):
        inward[p].wait()

        def widen(i, carry, p=p):
            i = i + p * (given // 128)
            t = table[here(i, 128), :].astype(F32)
            wide[pl.ds(8 + i * 256, 128, stride=2), :] = t[:, :LANES]
            wide[pl.ds(9 + i * 256, 128, stride=2), :] = t[:, LANES:]
            return carry

        lax.fori_loop(0, given // 128, widen, 0)

    for p in range(parts):

        def pick(owner, carry):
            for k in range(each):
                at = owner * each + k
                picked[pl.ds(at * 2, 2), :] = wide[pl.ds(ids_ref[owner, k] * 2 + 8, 2), :]
            return carry

        lax.fori_loop(p * taken, (p + 1) * taken, pick, 0)

        def join(i, carry):
            left = picked[pl.ds(i * 256, 128, stride=2), :]
            right = picked[pl.ds(i * 256 + 1, 128, stride=2), :]
            out[here(i, 128), :] = jnp.concatenate([left, right], axis=1).astype(BF)
            return carry

        lax.fori_loop(p * taken * each // 128, (p + 1) * taken * each // 128, join, 0)
        outward[p].start()
    for copy in outward:
        copy.wait()


def gather_call(ids, table, parts=8):
    rows, feat = table.shape
    count = ids.size
    return pl.pallas_call(
        functools.partial(gather_body, parts),
        in_specs=[whole_smem(), pl.BlockSpec(memory_space=pl.ANY)],
        out_specs=pl.BlockSpec(memory_space=pl.ANY),
        out_shape=jax.ShapeDtypeStruct((count, feat), BF),
        scratch_shapes=[
            pltpu.VMEM((rows, feat), BF),
            pltpu.VMEM((2 * rows + 8, LANES), F32),
            pltpu.VMEM((2 * count, LANES), F32),
            pltpu.VMEM((count, feat), BF),
            pltpu.SemaphoreType.DMA((2, parts)),
        ],
        compiler_params=params(60),
        name="gather_rows",
    )(ids, table)


def add_rows_body(unroll, given_parts, ids_ref, again_ref, clash_ref, *refs):
    given_refs, out_refs = refs[:given_parts], refs[given_parts:-3]
    total_a, total_b, wide = refs[-3:]
    count = sum(ref.shape[0] for ref in given_refs)
    part = out_refs[0].shape[0]
    rows = part * len(out_refs)

    def clear(i, carry):
        for total in (total_a, total_b):
            total[pl.ds(pl.multiple_of(i * 256, 256), 256), :] = jnp.zeros((256, LANES), F32)
        return carry

    lax.fori_loop(0, rows // 128, clear, 0)

    start = 0
    for ref in given_refs:

        def widen(i, carry, ref=ref, start=start):
            t = ref[pl.ds(pl.multiple_of(i * 128, 128), 128), :].astype(F32)
            wide[pl.ds(2 * start + i * 256, 128, stride=2), :] = t[:, :LANES]
            wide[pl.ds(2 * start + i * 256 + 1, 128, stride=2), :] = t[:, LANES:]
            return carry

        lax.fori_loop(0, ref.shape[0] // 128, widen, 0)
        start += ref.shape[0]

    def given(at):
        return wide[pl.ds(at * 2, 2), :]

    def add(i, carry):
        for total, base in ((total_a, i * 2 * unroll), (total_b, (i * 2 + 1) * unroll)):
            places = [pl.ds(ids_ref[base + k] * 2, 2) for k in range(unroll)]
            sums = [total[p, :] + given(base + k) for k, p in enumerate(places)]
            for p, v in zip(places, sums):
                total[p, :] = v
        return carry

    lax.fori_loop(0, count // (2 * unroll), add, 0)

    groups = count // unroll
    section = 16

    def check(i, carry):
        @pl.when(clash_ref[groups + i] != 0)
        def _():
            def add_again(j, inner):
                group = i * section + j

                @pl.when(clash_ref[group] != 0)
                def _():
                    for k in range(unroll):
                        p = pl.ds(again_ref[group * unroll + k] * 2, 2)
                        total_a[p, :] = total_a[p, :] + given(group * unroll + k)

                return inner

            lax.fori_loop(0, section, add_again, 0)

        return carry

    lax.fori_loop(0, groups // section, check, 0)

    for n, out_ref in enumerate(out_refs):

        def join(i, carry, n=n, out_ref=out_ref):
            left = pl.ds(n * part * 2 + i * 256, 128, stride=2)
            right = pl.ds(n * part * 2 + i * 256 + 1, 128, stride=2)
            both = [total_a[p, :] + total_b[p, :] for p in (left, right)]
            here = pl.ds(pl.multiple_of(i * 128, 128), 128)
            out_ref[here, :] = jnp.concatenate(both, axis=1).astype(out_ref.dtype)
            return carry

        lax.fori_loop(0, part // 128, join, 0)


def row_plan(ids, rows, unroll):
    grouped = ids.reshape(-1, unroll)
    spare = rows + lax.broadcasted_iota(jnp.int32, grouped.shape, 1)
    earlier = lax.broadcasted_iota(jnp.int32, (unroll, unroll), 1) < lax.broadcasted_iota(
        jnp.int32, (unroll, unroll), 0
    )
    same = (grouped[:, :, None] == grouped[:, None, :]) & earlier[None]
    twice = jnp.any(same, axis=2) & (grouped >= 0)
    once = jnp.where((grouped >= 0) & ~twice, grouped, spare)
    again = jnp.where(twice, grouped, spare)
    clash = jnp.any(twice, axis=1).astype(jnp.int32)
    sections = jnp.max(clash.reshape(-1, 16), axis=1)
    return once.reshape(-1), again.reshape(-1), jnp.concatenate([clash, sections])


def add_rows_call(plan, given, rows, unroll, parts):
    count, feat = sum(x.shape[0] for x in given), given[0].shape[1]
    return pl.pallas_call(
        functools.partial(add_rows_body, unroll, len(given)),
        in_specs=[whole_smem()] * 3 + [whole_vmem()] * len(given),
        out_specs=[whole_vmem()] * parts,
        out_shape=[jax.ShapeDtypeStruct((rows // parts, feat), BF)] * parts,
        scratch_shapes=[pltpu.VMEM((2 * (rows + unroll), LANES), F32)] * 2
        + [pltpu.VMEM((2 * count, LANES), F32)],
        compiler_params=params(48),
        name="add_rows",
        cost_estimate=pl.CostEstimate(flops=0, bytes_accessed=0, transcendentals=0),
    )(*plan, *given)


def gradients_body(
    d_inputs_ref,
    hist_ref,
    search_ref,
    mean_ref,
    word_mean_ref,
    dense_ref,
    act1_ref,
    act2_ref,
    d_pre1_ref,
    d_pre2_ref,
    d_user_ref,
    loss_ref,
    b1_ref,
    b2_ref,
    hot_counts_ref,
    word_counts_ref,
    hot_ref,
    word_ref,
    g1_ref,
    g2_ref,
    g3_ref,
    hot_part,
    word_part,
):
    step = pl.program_id(0)
    feat = hot_part.shape[1]

    @pl.when(step == 0)
    def _():
        hot_part[...] = (d_inputs_ref[:, :feat] / hist_ref[...]).astype(BF)
        word_part[...] = (d_inputs_ref[:, feat:] / search_ref[...]).astype(BF)

    for counts_ref, part, out_ref in (
        (hot_counts_ref, hot_part, hot_ref),
        (word_counts_ref, word_part, word_ref),
    ):
        out_ref[...] = left_product(counts_ref[...].astype(BF), part[...]).astype(BF)

    half = g1_ref.shape[1] // 2
    for k in range(2):

        @pl.when(step == k)
        def _(k=k):
            columns = slice(k * half, (k + 1) * half)
            start = 0
            for given_ref in (mean_ref, word_mean_ref, dense_ref):
                end = start + given_ref.shape[1]
                grad = left_product(given_ref[...], d_pre1_ref[:, columns])
                g1_ref[start:end, columns] = grad.astype(BF)
                start = end

    @pl.when(step == 2)
    def _():
        g2_ref[...] = left_product(act1_ref[...], d_pre2_ref[...]).astype(BF)

    @pl.when(step == 3)
    def _():
        d_user = d_user_ref[...]
        rows = act2_ref.shape[1]
        g3_ref[:rows, :] = left_product(act2_ref[...], d_user).astype(BF)
        b3 = jnp.sum(d_user.astype(F32), axis=0, keepdims=True)
        small = [
            x[:, i : i + feat]
            for x in (loss_ref[...], b1_ref[...], b2_ref[...], b3)
            for i in range(0, x.shape[1], feat)
        ]
        spare = g3_ref.shape[0] - rows - len(small)
        small.append(jnp.zeros((spare, feat), F32))
        g3_ref[rows:, :] = jnp.concatenate(small, axis=0).astype(BF)


def gradients_call(
    d_inputs, lengths, inputs, act1, act2, d_pre1, d_pre2, d_user, loss, b1, b2, counts
):
    hot_counts, word_counts = counts
    n, feat = d_user.shape
    steps = 4
    small = sum(x.shape[1] // feat for x in (loss, b1, b2, d_user))
    counts_spec = lambda c: pl.BlockSpec((n, c.shape[1] // steps), lambda i: (0, i))
    rows_spec = lambda c: pl.BlockSpec((c.shape[1] // steps, feat), lambda i: (i, 0))
    shapes = [
        (hot_counts.shape[1], feat),
        (word_counts.shape[1], feat),
        (sum(x.shape[1] for x in inputs), d_pre1.shape[1]),
        (act1.shape[1], d_pre2.shape[1]),
        (act2.shape[1] + small + -small % 16, feat),
    ]
    return pl.pallas_call(
        gradients_body,
        grid=(steps,),
        in_specs=[whole_vmem()] * (11 + len(inputs)) + [counts_spec(hot_counts), counts_spec(word_counts)],
        out_specs=[rows_spec(hot_counts), rows_spec(word_counts)] + [whole_vmem()] * 3,
        out_shape=[jax.ShapeDtypeStruct(x, BF) for x in shapes],
        scratch_shapes=[pltpu.VMEM((n, feat), BF)] * 2,
        compiler_params=params(50),
        name="gradients",
    )(
        d_inputs, *lengths, *inputs, act1, act2, d_pre1, d_pre2, d_user, loss, b1, b2, *counts
    )


def slot_spread_body(cuts, counts_ref, length_ref, d_inputs_ref, *refs):
    out_refs, part_ref = refs[:-1], refs[-1]
    feat = part_ref.shape[1]

    @pl.when(pl.program_id(0) == 0)
    def _():
        part_ref[...] = (d_inputs_ref[:, :feat] / length_ref[...]).astype(BF)

    grad = left_product(counts_ref[...].astype(BF), part_ref[...])
    grad = grad.reshape(-1, sum(cuts), feat)
    start = 0
    for ref, cut in zip(out_refs, cuts):
        ref[...] = grad[:, start : start + cut, :].astype(BF)
        start += cut


def slot_spread_call(counts, lengths, d_inputs, feat, cuts, steps):
    n, slots = counts.shape
    owners = slots // sum(cuts)
    return pl.pallas_call(
        functools.partial(slot_spread_body, cuts),
        grid=(steps,),
        in_specs=[pl.BlockSpec((n, slots // steps), lambda i: (0, i)), whole_vmem(), whole_vmem()],
        out_specs=[pl.BlockSpec((owners // steps, cut, feat), lambda i: (i, 0, 0)) for cut in cuts],
        out_shape=[jax.ShapeDtypeStruct((owners, cut, feat), BF) for cut in cuts],
        scratch_shapes=[pltpu.VMEM((n, feat), BF)],
        compiler_params=params(60),
        cost_estimate=pl.CostEstimate(flops=0, bytes_accessed=0, transcendentals=0),
        name="slot_spread",
    )(counts, lengths, d_inputs)


def widen_body(blocked, losses, examples, *refs):
    given, outs = refs[: blocked + 2], refs[blocked + 2 :]
    for x_ref, out_ref in zip(given[:blocked], outs[:blocked]):
        out_ref[...] = x_ref[...].astype(F32)
    first_ref, last_ref = given[blocked:]
    first_out_ref, last_out_ref, loss_ref, *bias_refs = outs[blocked:]

    @pl.when(pl.program_id(0) == 0)
    def _():
        rows, feat = last_out_ref.shape
        first_out_ref[...] = first_ref[...].astype(F32)[: first_out_ref.shape[0], :]
        last_out_ref[...] = last_ref[:rows, :].astype(F32)
        small = last_ref[rows:, :].astype(F32)
        start = losses
        loss_ref[...] = jnp.sum(small[:start], keepdims=True) / examples
        for ref in bias_refs:
            for i in range(ref.shape[1] // feat):
                ref[:, i * feat : (i + 1) * feat] = small[start : start + 1]
                start += 1


def widen_call(arrays, first, last, first_rows, last_rows, loss_rows, widths, examples, steps):
    feat = last.shape[1]
    spec = lambda a: pl.BlockSpec((a.shape[0] // steps, a.shape[1]), lambda i: (i, 0))
    shapes = [a.shape for a in arrays]
    shapes += [(first_rows, first.shape[1]), (last_rows, feat), (1, 1)] + [(1, w) for w in widths]
    return pl.pallas_call(
        functools.partial(widen_body, len(arrays), loss_rows, examples),
        grid=(steps,),
        in_specs=[spec(a) for a in arrays] + [whole_vmem()] * 2,
        out_specs=[spec(a) for a in arrays] + [whole_vmem()] * (len(shapes) - len(arrays)),
        out_shape=[jax.ShapeDtypeStruct(s, F32) for s in shapes],
        compiler_params=params(60),
        name="widen",
    )(*arrays, first, last)


def add_parts_body(*refs):
    count = len(refs) // 2
    for k in range(count):

        @pl.when(pl.program_id(0) == k)
        def _(k=k):
            refs[-1][...] = refs[k][...].astype(F32) + refs[count + k][...].astype(F32)


def add_pair_call(own, others):
    rows, feat = own[0].shape
    spec = pl.BlockSpec((rows, feat), lambda i: (0, 0))
    return pl.pallas_call(
        add_parts_body,
        grid=(len(own),),
        in_specs=[spec] * (2 * len(own)),
        out_specs=pl.BlockSpec((rows, feat), lambda i: (i, 0)),
        out_shape=jax.ShapeDtypeStruct((rows * len(own), feat), F32),
        compiler_params=params(60),
        cost_estimate=pl.CostEstimate(flops=0, bytes_accessed=0, transcendentals=0),
        name="add_parts",
    )(*own, *others)


def softmax_body(
    inv_count,
    chunk,
    mask_hbm,
    table_hbm,
    table_t_hbm,
    user_t_ref,
    label_ref,
    d_user_ref,
    grad_ref,
    loss_ref,
    logits,
    grad_sum,
    mask_ref,
    table_ref,
    table_t_ref,
    sems,
):
    rows, feat = table_ref.shape
    block = user_t_ref.shape[1]
    chunks = rows // chunk
    step = pl.program_id(0)
    last = pl.num_programs(0) - 1

    def at(c):
        return pl.ds(pl.multiple_of(c * chunk, chunk), chunk)

    def fetches(c):
        return (
            pltpu.make_async_copy(table_hbm.at[at(c)], table_ref.at[at(c)], sems.at[0, c]),
            pltpu.make_async_copy(mask_hbm.at[at(c)], mask_ref.at[at(c)], sems.at[1, c]),
        )

    turned = pltpu.make_async_copy(table_t_hbm, table_t_ref, sems.at[2, 0])

    @pl.when(step == 0)
    def _():
        for c in range(chunks):
            for fetch in fetches(c):
                fetch.start()
        turned.start()

    label = label_ref[...]
    user_t = user_t_ref[...]
    user = user_t.astype(F32).T.astype(BF)
    sublane = lax.broadcasted_iota(jnp.int32, (8, block), 0)

    def hits(c):
        place = label - c * chunk - sublane
        return jnp.concatenate([place == 8 * g for g in range(chunk // 8)], axis=0)


    def fold(v, op):
        return op(v.reshape(chunk // 8, 8, block), axis=0)

    def first(c, carry):
        @pl.when(step == 0)
        def _():
            for fetch in fetches(c):
                fetch.wait()

        peak, pos = carry
        s = jnp.dot(table_ref[at(c), :], user_t, preferred_element_type=F32)
        pos = pos + fold(jnp.where(hits(c), s, 0.0), jnp.sum)
        s = s + jnp.concatenate([mask_ref[at(c), :]] * (block // LANES), axis=1)
        logits[at(c), :] = s
        return jnp.maximum(peak, fold(s, jnp.max)), pos

    peak, pos = lax.fori_loop(
        0,
        chunks,
        first,
        (jnp.full((8, block), -jnp.inf, F32), jnp.zeros((8, block), F32)),
    )
    pos = jnp.sum(pos, axis=0, keepdims=True)
    peak = jnp.maximum(jnp.max(peak, axis=0, keepdims=True), pos)

    def second(c, total):
        p = jnp.exp(logits[at(c), :] - peak)
        logits[at(c), :] = p
        return total + fold(p, jnp.sum)

    total = lax.fori_loop(0, chunks, second, jnp.zeros((8, block), F32))
    pos_exp = jnp.exp(pos - peak)
    total = jnp.sum(total, axis=0, keepdims=True) + pos_exp
    loss_ref[...] = peak + jnp.log(total) - pos
    scale = inv_count / total
    d_pos = (pos_exp / total - 1.0) * inv_count

    @pl.when(step == 0)
    def _():
        turned.wait()

    def back(add, store):
        def third(c, d_user_t):
            d = logits[at(c), :] * scale
            d = jnp.where(hits(c), d + d_pos, d).astype(BF)
            term = jnp.dot(d, user, preferred_element_type=F32)
            if add:
                term = grad_sum[at(c), :] + term
            if store:
                grad_ref[at(c), :] = term.astype(BF)
            else:
                grad_sum[at(c), :] = term
            return d_user_t + jnp.dot(table_t_ref[:, at(c)], d, preferred_element_type=F32)

        d_user_t = lax.fori_loop(0, chunks, third, jnp.zeros((feat, block), F32))
        d_user_ref[...] = d_user_t.T.astype(BF)

    @pl.when(step == 0)
    def _():
        back(False, False)

    @pl.when((step > 0) & (step < last))
    def _():
        back(True, False)

    @pl.when(step == last)
    def _():
        back(True, True)


def softmax_call(mask, table, table_t, user, labels, block=512, chunk=4096):
    n, feat = user.shape
    rows = table.shape[0]
    across = lambda h: pl.BlockSpec((h, block), lambda i: (0, i))
    any_place = pl.BlockSpec(memory_space=pl.ANY)
    return pl.pallas_call(
        functools.partial(softmax_body, 1.0 / n, chunk),
        grid=(n // block,),
        in_specs=[any_place] * 3
        + [across(feat), across(1)],
        out_specs=[pl.BlockSpec((block, feat), lambda i: (i, 0)), whole_vmem(), across(1)],
        out_shape=[
            jax.ShapeDtypeStruct((n, feat), BF),
            jax.ShapeDtypeStruct((rows, feat), BF),
            jax.ShapeDtypeStruct((1, n), F32),
        ],
        scratch_shapes=[
            pltpu.VMEM((rows, block), F32),
            pltpu.VMEM((rows, feat), F32),
            pltpu.VMEM((rows, LANES), F32),
            pltpu.VMEM((rows, feat), BF),
            pltpu.VMEM((feat, rows), BF),
            pltpu.SemaphoreType.DMA((3, rows // chunk)),
        ],
        compiler_params=params(46),
        name="sampled_softmax",
    )(mask, table, table_t, user.T, labels.reshape(1, n))


def sampled_mask(negatives, rows):
    high = lax.broadcasted_iota(jnp.int32, (rows // LANES, negatives.shape[0]), 0)
    low = lax.broadcasted_iota(jnp.int32, (LANES, negatives.shape[0]), 0)
    high_hot = (high == negatives[None, :] // LANES).astype(BF)
    low_hot = (low == negatives[None, :] % LANES).astype(BF)
    sampled = right_product(high_hot, low_hot).reshape(rows, 1)
    return jnp.broadcast_to(jnp.where(sampled > 0.5, F32(0.0), F32(-1e30)), (rows, LANES))


def left_product(first_op, second_op):
    return lax.dot_general(
        first_op, second_op, (((0,), (0,)), ((), ())), preferred_element_type=F32
    )


def right_product(first_op, second_op):
    return lax.dot_general(
        first_op, second_op, (((1,), (1,)), ((), ())), preferred_element_type=F32
    )


def gelu_back(pre_value, d_act):
    unused, pull = jax.vjp(jax.nn.gelu, pre_value)
    return pull(d_act)[0]


def in_range_ids(ids, lengths, offset):
    slot = lax.broadcasted_iota(jnp.int32, ids.shape, 1)
    kept = jnp.where(slot < lengths[:, None], ids + offset, -1)
    return jnp.pad(kept, ((0, 0), (0, LANES // 2 - ids.shape[1])), constant_values=-1)


def local(
    hot_table,
    tail_table,
    word_table,
    out_table,
    w_first,
    b_first,
    w_second,
    b_second,
    w_third,
    b_third,
    dense_feats,
    hist_ids,
    hist_len,
    search_ids,
    search_len,
    requests,
    labels,
    negatives,
):
    feat = hot_table.shape[1]
    hot_rows = hot_table.shape[0]
    owners, per_owner = requests.shape
    slots = owners * per_owner
    examples_dev = hist_ids.shape[0]
    examples_all = examples_dev * lax.axis_size("group") * lax.axis_size("wide")
    shard_rows = tail_table.shape[0]
    hist_float = hist_len[:, None].astype(F32)
    search_float = search_len[:, None].astype(F32)

    asked = lax.all_to_all(requests, "wide", split_axis=0, concat_axis=0, tiled=True)
    looked = gather_call(asked, tail_table)
    returned = lax.all_to_all(
        looked.reshape(owners, per_owner, feat), "wide", split_axis=0, concat_axis=0, tiled=True
    ).reshape(slots, feat)

    asked, negatives, looked = lax.optimization_barrier((asked, negatives, looked))
    ids = jnp.concatenate(
        [
            in_range_ids(hist_ids, hist_len, 0),
            in_range_ids(search_ids, search_len, hot_rows + slots),
        ],
        axis=1,
    )
    out_table_t = out_table.T
    mask = sampled_mask(negatives, out_table.shape[0])
    unroll = 16
    cuts = (16, 16, 16, 32, 16, 16, 16)
    edges = [sum(cuts[:i]) for i in range(len(cuts) + 1)]
    asked_parts = [asked[:, i:j].reshape(-1) for i, j in zip(edges, edges[1:])]
    plan = row_plan(jnp.concatenate(asked_parts), shard_rows, unroll)
    ids, out_table_t, mask, plan, looked = lax.optimization_barrier(
        (ids, out_table_t, mask, plan, looked)
    )
    hot_counts, slot_counts, word_counts, hot_sum, word_sum = counts_call(
        ids, hot_table, word_table, slots
    )

    hist_mean = (hot_sum + jnp.dot(slot_counts.astype(BF), returned, preferred_element_type=F32)) / hist_float
    search_mean = word_sum / search_float
    hist_mean, search_mean = hist_mean.astype(BF), search_mean.astype(BF)
    dense = jnp.pad(dense_feats, ((0, 0), (0, -w_first.shape[0] % LANES)))
    inputs = jnp.concatenate([hist_mean, search_mean, dense_feats], axis=1)
    pre_first = jnp.dot(inputs, w_first, preferred_element_type=F32) + b_first.astype(F32)
    act_first = jax.nn.gelu(pre_first).astype(BF)
    pre_second = jnp.dot(act_first, w_second, preferred_element_type=F32) + b_second.astype(F32)
    act_second = jax.nn.gelu(pre_second).astype(BF)
    user = (jnp.dot(act_second, w_third, preferred_element_type=F32) + b_third.astype(F32)).astype(
        BF
    )

    d_user, out_grad, per_example = softmax_call(mask, out_table, out_table_t, user, labels)
    d_pre_second = gelu_back(pre_second, right_product(d_user, w_third)).astype(BF)
    d_pre_first = gelu_back(pre_first, right_product(d_pre_second, w_second)).astype(BF)
    d_inputs = right_product(d_pre_first, w_first[: 2 * feat])

    packed = gradients_call(
        d_inputs,
        (hist_float, search_float),
        (hist_mean, search_mean, dense),
        act_first,
        act_second,
        d_pre_first,
        d_pre_second,
        d_user,
        per_example,
        jnp.sum(d_pre_first.astype(F32), axis=0)[None],
        jnp.sum(d_pre_second.astype(F32), axis=0)[None],
        (hot_counts, word_counts),
    )
    packed = (*packed, out_grad)
    w3_rows = w_third.shape[0]
    packed, slot_counts = lax.optimization_barrier((packed, slot_counts))
    summed = lax.psum(packed, ("group", "wide"))

    slot_grads = slot_spread_call(slot_counts, hist_float, d_inputs, feat, cuts, 4)
    owed = []
    for part in slot_grads:
        if owed:
            part, owed[-1] = lax.optimization_barrier((part, owed[-1]))
        owed.append(lax.all_to_all(part, "wide", split_axis=0, concat_axis=0, tiled=True))
    owed = [x.reshape(-1, feat) for x in owed]
    own = add_rows_call(plan, owed, shard_rows, unroll, 4)
    others = [lax.ppermute(x, "group", [(0, 1), (1, 0)]) for x in own]
    tail_grad = add_pair_call(own, others)
    summed, tail_grad = lax.optimization_barrier((summed, tail_grad))
    hot_all, word_all, out_all, w2_all, w1_all, w3_all, loss_value, b1_all, b2_all, b3_all = widen_call(
        (summed[0], summed[1], summed[5], summed[3]),
        summed[2],
        summed[4],
        w_first.shape[0],
        w3_rows,
        examples_dev // feat,
        (b_first.shape[0], b_second.shape[0], b_third.shape[0]),
        examples_all,
        4,
    )
    return (
        loss_value[0, 0],
        hot_all,
        tail_grad,
        word_all,
        out_all,
        w1_all,
        b1_all[0],
        w2_all,
        b2_all[0],
        w3_all,
        b3_all[0],
    )


def solution(mesh):
    split = ("group", "wide")
    in_specs = (
        (P(), P("wide", None))
        + (P(),) * 8
        + (P(split, None), P(split, None), P(split), P(split, None), P(split), P(split, None))
        + (P(split), P())
    )
    out_specs = (P(), P(), P("wide", None)) + (P(),) * 8
    return jax.shard_map(local, mesh=mesh, in_specs=in_specs, out_specs=out_specs, check_vma=False)
```

```python
import functools

import jax
import jax.numpy as jnp
from jax import lax
from jax.experimental import pallas as pl
from jax.experimental.pallas import tpu as pltpu
from jax.sharding import PartitionSpec as P

BF = jnp.bfloat16
F32 = jnp.float32
LANES = 128
MIB = 1024 * 1024


def params(mib):
    return pltpu.CompilerParams(vmem_limit_bytes=mib * MIB)


def whole_vmem():
    return pl.BlockSpec(memory_space=pltpu.VMEM)


def whole_smem():
    return pl.BlockSpec(memory_space=pltpu.SMEM)


def counts_body(cuts, ids_ref, hot_ref, word_ref, *refs):
    count_refs = refs[: len(cuts)]
    hist_ref, word_sum_ref, scratch, low_ref, high_ref = refs[len(cuts) :]
    block = ids_ref.shape[0]
    groups = sum(cuts)
    rows = groups + 8
    ids = ids_ref[...]
    low_ref[...] = (ids & (LANES - 1)).astype(F32)
    place = lax.broadcasted_iota(jnp.int32, ids.shape, 0) & 7
    high_ref[...] = (jnp.where(ids < 0, -64, ids >> 7) + place).astype(F32)
    low_iota = lax.broadcasted_iota(jnp.int32, (LANES, LANES), 0).astype(BF)
    high_iota = lax.broadcasted_iota(jnp.int32, (rows, LANES), 0).astype(BF)
    one = jnp.ones((), BF)
    zero = jnp.zeros((), BF)
    unroll = block

    def build(i, carry):
        for k in range(unroll):
            e = i * unroll + k
            low = jnp.broadcast_to(low_ref[pl.ds(e, 1), :], (LANES, LANES)).astype(BF)
            high = jnp.broadcast_to(high_ref[pl.ds(e, 1), :], (rows, LANES)).astype(BF)
            low_hot = jnp.where(low_iota == low, one, zero)
            high_hot = jnp.where(high_iota == high, one, zero)
            scratch[pl.ds(pl.multiple_of(e * rows, 8), rows), :] = right_product(high_hot, low_hot)
        return carry

    lax.fori_loop(0, block // unroll, build, 0)

    def regroup(i, carry):
        here = pl.ds(pl.multiple_of(i * 32, 32), 32)
        g = 0
        for ref, cut in zip(count_refs, cuts):
            for c in range(cut):
                eights = [
                    scratch[pl.ds((i * 32 + e) * rows + g, 8, stride=rows + 1), :]
                    for e in range(0, 32, 8)
                ]
                ref[here, c * LANES : (c + 1) * LANES] = jnp.concatenate(eights, axis=0).astype(
                    jnp.int8
                )
                g += 1
        return carry

    lax.fori_loop(0, block // 32, regroup, 0)
    hist_ref[...] = jnp.dot(count_refs[0][...].astype(BF), hot_ref[...], preferred_element_type=F32)
    word_sum_ref[...] = jnp.dot(
        count_refs[-1][...].astype(BF), word_ref[...], preferred_element_type=F32
    )


def counts_call(ids, hot, word, tail_rows, block=128):
    n = ids.shape[0]
    feat = hot.shape[1]
    widths = (hot.shape[0], tail_rows, word.shape[0])
    cuts = tuple(w // LANES for w in widths)
    rows_of = lambda w: pl.BlockSpec((block, w), lambda i: (i, 0))
    fixed = lambda s: pl.BlockSpec(s, lambda i: (0, 0))
    return pl.pallas_call(
        functools.partial(counts_body, cuts),
        grid=(n // block,),
        in_specs=[rows_of(LANES), fixed(hot.shape), fixed(word.shape)],
        out_specs=[rows_of(w) for w in widths] + [rows_of(feat)] * 2,
        out_shape=[jax.ShapeDtypeStruct((n, w), jnp.int8) for w in widths]
        + [jax.ShapeDtypeStruct((n, feat), F32)] * 2,
        scratch_shapes=[pltpu.VMEM((block * (sum(cuts) + 8), LANES), F32)]
        + [pltpu.VMEM((block, LANES), F32)] * 2,
        compiler_params=params(56),
        name="counts",
    )(ids, hot, word)


def gather_body(parts, ids_ref, table_hbm, out_hbm, table, wide, picked, out, sems):
    rows = table.shape[0]
    owners, each = ids_ref.shape
    here = lambda i, size: pl.ds(pl.multiple_of(i * size, size), size)
    given = rows // parts
    taken = owners // parts
    inward = [
        pltpu.make_async_copy(
            table_hbm.at[here(p, given)], table.at[here(p, given)], sems.at[0, p]
        )
        for p in range(parts)
    ]
    outward = [
        pltpu.make_async_copy(
            out.at[here(p, taken * each)], out_hbm.at[here(p, taken * each)], sems.at[1, p]
        )
        for p in range(parts)
    ]
    for copy in inward:
        copy.start()
    wide[:8, :] = jnp.zeros((8, LANES), F32)
    for p in range(parts):
        inward[p].wait()

        def widen(i, carry, p=p):
            i = i + p * (given // 128)
            t = table[here(i, 128), :].astype(F32)
            wide[pl.ds(8 + i * 256, 128, stride=2), :] = t[:, :LANES]
            wide[pl.ds(9 + i * 256, 128, stride=2), :] = t[:, LANES:]
            return carry

        lax.fori_loop(0, given // 128, widen, 0)

    for p in range(parts):

        def pick(owner, carry):
            for k in range(each):
                at = owner * each + k
                picked[pl.ds(at * 2, 2), :] = wide[pl.ds(ids_ref[owner, k] * 2 + 8, 2), :]
            return carry

        lax.fori_loop(p * taken, (p + 1) * taken, pick, 0)

        def join(i, carry):
            left = picked[pl.ds(i * 256, 128, stride=2), :]
            right = picked[pl.ds(i * 256 + 1, 128, stride=2), :]
            out[here(i, 128), :] = jnp.concatenate([left, right], axis=1).astype(BF)
            return carry

        lax.fori_loop(p * taken * each // 128, (p + 1) * taken * each // 128, join, 0)
        outward[p].start()
    for copy in outward:
        copy.wait()


def gather_call(ids, table, parts=8):
    rows, feat = table.shape
    count = ids.size
    return pl.pallas_call(
        functools.partial(gather_body, parts),
        in_specs=[whole_smem(), pl.BlockSpec(memory_space=pl.ANY)],
        out_specs=pl.BlockSpec(memory_space=pl.ANY),
        out_shape=jax.ShapeDtypeStruct((count, feat), BF),
        scratch_shapes=[
            pltpu.VMEM((rows, feat), BF),
            pltpu.VMEM((2 * rows + 8, LANES), F32),
            pltpu.VMEM((2 * count, LANES), F32),
            pltpu.VMEM((count, feat), BF),
            pltpu.SemaphoreType.DMA((2, parts)),
        ],
        compiler_params=params(60),
        name="gather_rows",
    )(ids, table)


def add_rows_body(unroll, given_parts, ids_ref, again_ref, clash_ref, *refs):
    given_refs, out_refs = refs[:given_parts], refs[given_parts:-3]
    total_a, total_b, wide = refs[-3:]
    count = sum(ref.shape[0] for ref in given_refs)
    part = out_refs[0].shape[0]
    rows = part * len(out_refs)

    def clear(i, carry):
        for total in (total_a, total_b):
            total[pl.ds(pl.multiple_of(i * 256, 256), 256), :] = jnp.zeros((256, LANES), F32)
        return carry

    lax.fori_loop(0, rows // 128, clear, 0)

    start = 0
    for ref in given_refs:

        def widen(i, carry, ref=ref, start=start):
            t = ref[pl.ds(pl.multiple_of(i * 128, 128), 128), :].astype(F32)
            wide[pl.ds(2 * start + i * 256, 128, stride=2), :] = t[:, :LANES]
            wide[pl.ds(2 * start + i * 256 + 1, 128, stride=2), :] = t[:, LANES:]
            return carry

        lax.fori_loop(0, ref.shape[0] // 128, widen, 0)
        start += ref.shape[0]

    def given(at):
        return wide[pl.ds(at * 2, 2), :]

    def add(i, carry):
        for total, base in ((total_a, i * 2 * unroll), (total_b, (i * 2 + 1) * unroll)):
            places = [pl.ds(ids_ref[base + k] * 2, 2) for k in range(unroll)]
            sums = [total[p, :] + given(base + k) for k, p in enumerate(places)]
            for p, v in zip(places, sums):
                total[p, :] = v
        return carry

    lax.fori_loop(0, count // (2 * unroll), add, 0)

    groups = count // unroll
    section = 16

    def check(i, carry):
        @pl.when(clash_ref[groups + i] != 0)
        def _():
            def add_again(j, inner):
                group = i * section + j

                @pl.when(clash_ref[group] != 0)
                def _():
                    for k in range(unroll):
                        p = pl.ds(again_ref[group * unroll + k] * 2, 2)
                        total_a[p, :] = total_a[p, :] + given(group * unroll + k)

                return inner

            lax.fori_loop(0, section, add_again, 0)

        return carry

    lax.fori_loop(0, groups // section, check, 0)

    for n, out_ref in enumerate(out_refs):

        def join(i, carry, n=n, out_ref=out_ref):
            left = pl.ds(n * part * 2 + i * 256, 128, stride=2)
            right = pl.ds(n * part * 2 + i * 256 + 1, 128, stride=2)
            both = [total_a[p, :] + total_b[p, :] for p in (left, right)]
            here = pl.ds(pl.multiple_of(i * 128, 128), 128)
            out_ref[here, :] = jnp.concatenate(both, axis=1).astype(out_ref.dtype)
            return carry

        lax.fori_loop(0, part // 128, join, 0)


def row_plan(ids, rows, unroll):
    grouped = ids.reshape(-1, unroll)
    spare = rows + lax.broadcasted_iota(jnp.int32, grouped.shape, 1)
    earlier = lax.broadcasted_iota(jnp.int32, (unroll, unroll), 1) < lax.broadcasted_iota(
        jnp.int32, (unroll, unroll), 0
    )
    same = (grouped[:, :, None] == grouped[:, None, :]) & earlier[None]
    twice = jnp.any(same, axis=2) & (grouped >= 0)
    once = jnp.where((grouped >= 0) & ~twice, grouped, spare)
    again = jnp.where(twice, grouped, spare)
    clash = jnp.any(twice, axis=1).astype(jnp.int32)
    sections = jnp.max(clash.reshape(-1, 16), axis=1)
    return once.reshape(-1), again.reshape(-1), jnp.concatenate([clash, sections])


def add_rows_call(plan, given, rows, unroll, parts):
    count, feat = sum(x.shape[0] for x in given), given[0].shape[1]
    return pl.pallas_call(
        functools.partial(add_rows_body, unroll, len(given)),
        in_specs=[whole_smem()] * 3 + [whole_vmem()] * len(given),
        out_specs=[whole_vmem()] * parts,
        out_shape=[jax.ShapeDtypeStruct((rows // parts, feat), BF)] * parts,
        scratch_shapes=[pltpu.VMEM((2 * (rows + unroll), LANES), F32)] * 2
        + [pltpu.VMEM((2 * count, LANES), F32)],
        compiler_params=params(48),
        name="add_rows",
        cost_estimate=pl.CostEstimate(flops=0, bytes_accessed=0, transcendentals=0),
    )(*plan, *given)


def gradients_body(
    d_inputs_ref,
    hist_ref,
    search_ref,
    mean_ref,
    word_mean_ref,
    dense_ref,
    act1_any,
    act2_any,
    d_pre1_any,
    d_pre2_any,
    d_user_ref,
    loss_ref,
    b1_ref,
    b2_ref,
    hot_counts_ref,
    word_counts_ref,
    hot_ref,
    word_ref,
    g1_ref,
    g2_ref,
    g3_ref,
    hot_part,
    word_part,
    act1_ref,
    act2_ref,
    d_pre1_ref,
    d_pre2_ref,
    sems,
):
    step = pl.program_id(0)
    feat = hot_part.shape[1]
    pairs = (
        (act1_any, act1_ref),
        (act2_any, act2_ref),
        (d_pre2_any, d_pre2_ref),
        (d_pre1_any, d_pre1_ref),
    )
    fetches = [pltpu.make_async_copy(x, y, sems.at[i]) for i, (x, y) in enumerate(pairs)]

    @pl.when(step == 0)
    def _():
        for fetch in fetches:
            fetch.start()
        hot_part[...] = (d_inputs_ref[:, :feat] / hist_ref[...]).astype(BF)
        word_part[...] = (d_inputs_ref[:, feat:] / search_ref[...]).astype(BF)

    for counts_ref, part, out_ref in (
        (hot_counts_ref, hot_part, hot_ref),
        (word_counts_ref, word_part, word_ref),
    ):
        out_ref[...] = left_product(counts_ref[...].astype(BF), part[...]).astype(BF)

    @pl.when(step == 1)
    def _():
        for fetch in fetches[:3]:
            fetch.wait()
        g2_ref[...] = left_product(act1_ref[...], d_pre2_ref[...]).astype(BF)
        d_user = d_user_ref[...]
        rows = act2_ref.shape[1]
        g3_ref[:rows, :] = left_product(act2_ref[...], d_user).astype(BF)
        b3 = jnp.sum(d_user.astype(F32), axis=0, keepdims=True)
        small = [
            x[:, i : i + feat]
            for x in (loss_ref[...], b1_ref[...], b2_ref[...], b3)
            for i in range(0, x.shape[1], feat)
        ]
        spare = g3_ref.shape[0] - rows - len(small)
        small.append(jnp.zeros((spare, feat), F32))
        g3_ref[rows:, :] = jnp.concatenate(small, axis=0).astype(BF)

    half = g1_ref.shape[1] // 2
    for k in range(2):

        @pl.when(step == 2 + k)
        def _(k=k):
            if k == 0:
                fetches[3].wait()
            columns = slice(k * half, (k + 1) * half)
            start = 0
            for given_ref in (mean_ref, word_mean_ref, dense_ref):
                end = start + given_ref.shape[1]
                grad = left_product(given_ref[...], d_pre1_ref[:, columns])
                g1_ref[start:end, columns] = grad.astype(BF)
                start = end


def gradients_call(
    d_inputs, lengths, inputs, act1, act2, d_pre1, d_pre2, d_user, loss, b1, b2, counts
):
    hot_counts, word_counts = counts
    n, feat = d_user.shape
    steps = 4
    small = sum(x.shape[1] // feat for x in (loss, b1, b2, d_user))
    counts_spec = lambda c: pl.BlockSpec((n, c.shape[1] // steps), lambda i: (0, i))
    rows_spec = lambda c: pl.BlockSpec((c.shape[1] // steps, feat), lambda i: (i, 0))
    shapes = [
        (hot_counts.shape[1], feat),
        (word_counts.shape[1], feat),
        (sum(x.shape[1] for x in inputs), d_pre1.shape[1]),
        (act1.shape[1], d_pre2.shape[1]),
        (act2.shape[1] + small + -small % 16, feat),
    ]
    return pl.pallas_call(
        gradients_body,
        grid=(steps,),
        in_specs=[whole_vmem()] * (3 + len(inputs))
        + [pl.BlockSpec(memory_space=pl.ANY)] * 4
        + [whole_vmem()] * 4
        + [counts_spec(hot_counts), counts_spec(word_counts)],
        out_specs=[rows_spec(hot_counts), rows_spec(word_counts)] + [whole_vmem()] * 3,
        out_shape=[jax.ShapeDtypeStruct(x, BF) for x in shapes],
        scratch_shapes=[pltpu.VMEM((n, feat), BF)] * 2
        + [pltpu.VMEM(x.shape, BF) for x in (act1, act2, d_pre1, d_pre2)]
        + [pltpu.SemaphoreType.DMA((4,))],
        compiler_params=params(50),
        name="gradients",
    )(
        d_inputs, *lengths, *inputs, act1, act2, d_pre1, d_pre2, d_user, loss, b1, b2, *counts
    )


def slot_spread_body(cuts, counts_ref, length_ref, d_inputs_ref, *refs):
    out_refs, part_ref = refs[:-1], refs[-1]
    feat = part_ref.shape[1]

    @pl.when(pl.program_id(0) == 0)
    def _():
        part_ref[...] = (d_inputs_ref[:, :feat] / length_ref[...]).astype(BF)

    grad = left_product(counts_ref[...].astype(BF), part_ref[...])
    grad = grad.reshape(-1, sum(cuts), feat)
    start = 0
    for ref, cut in zip(out_refs, cuts):
        ref[...] = grad[:, start : start + cut, :].astype(BF)
        start += cut


def slot_spread_call(counts, lengths, d_inputs, feat, cuts, steps):
    n, slots = counts.shape
    owners = slots // sum(cuts)
    return pl.pallas_call(
        functools.partial(slot_spread_body, cuts),
        grid=(steps,),
        in_specs=[pl.BlockSpec((n, slots // steps), lambda i: (0, i)), whole_vmem(), whole_vmem()],
        out_specs=[pl.BlockSpec((owners // steps, cut, feat), lambda i: (i, 0, 0)) for cut in cuts],
        out_shape=[jax.ShapeDtypeStruct((owners, cut, feat), BF) for cut in cuts],
        scratch_shapes=[pltpu.VMEM((n, feat), BF)],
        compiler_params=params(60),
        cost_estimate=pl.CostEstimate(flops=0, bytes_accessed=0, transcendentals=0),
        name="slot_spread",
    )(counts, lengths, d_inputs)


def widen_body(blocked, losses, examples, *refs):
    given, outs = refs[: blocked + 2], refs[blocked + 2 :]
    for x_ref, out_ref in zip(given[:blocked], outs[:blocked]):
        out_ref[...] = x_ref[...].astype(F32)
    first_ref, last_ref = given[blocked:]
    first_out_ref, last_out_ref, loss_ref, *bias_refs = outs[blocked:]

    @pl.when(pl.program_id(0) == 0)
    def _():
        rows, feat = last_out_ref.shape
        first_out_ref[...] = first_ref[...].astype(F32)[: first_out_ref.shape[0], :]
        last_out_ref[...] = last_ref[:rows, :].astype(F32)
        small = last_ref[rows:, :].astype(F32)
        start = losses
        loss_ref[...] = jnp.sum(small[:start], keepdims=True) / examples
        for ref in bias_refs:
            for i in range(ref.shape[1] // feat):
                ref[:, i * feat : (i + 1) * feat] = small[start : start + 1]
                start += 1


def widen_call(arrays, first, last, first_rows, last_rows, loss_rows, widths, examples, steps):
    feat = last.shape[1]
    spec = lambda a: pl.BlockSpec((a.shape[0] // steps, a.shape[1]), lambda i: (i, 0))
    shapes = [a.shape for a in arrays]
    shapes += [(first_rows, first.shape[1]), (last_rows, feat), (1, 1)] + [(1, w) for w in widths]
    return pl.pallas_call(
        functools.partial(widen_body, len(arrays), loss_rows, examples),
        grid=(steps,),
        in_specs=[spec(a) for a in arrays] + [whole_vmem()] * 2,
        out_specs=[spec(a) for a in arrays] + [whole_vmem()] * (len(shapes) - len(arrays)),
        out_shape=[jax.ShapeDtypeStruct(s, F32) for s in shapes],
        compiler_params=params(60),
        name="widen",
    )(*arrays, first, last)


def add_parts_body(*refs):
    count = len(refs) // 2
    for k in range(count):

        @pl.when(pl.program_id(0) == k)
        def _(k=k):
            refs[-1][...] = refs[k][...].astype(F32) + refs[count + k][...].astype(F32)


def add_pair_call(own, others):
    rows, feat = own[0].shape
    spec = pl.BlockSpec((rows, feat), lambda i: (0, 0))
    return pl.pallas_call(
        add_parts_body,
        grid=(len(own),),
        in_specs=[spec] * (2 * len(own)),
        out_specs=pl.BlockSpec((rows, feat), lambda i: (i, 0)),
        out_shape=jax.ShapeDtypeStruct((rows * len(own), feat), F32),
        compiler_params=params(60),
        cost_estimate=pl.CostEstimate(flops=0, bytes_accessed=0, transcendentals=0),
        name="add_parts",
    )(*own, *others)


def softmax_body(
    inv_count,
    chunk,
    mask_hbm,
    table_hbm,
    table_t_hbm,
    user_t_ref,
    label_ref,
    d_user_ref,
    grad_ref,
    loss_ref,
    logits,
    grad_sum,
    mask_ref,
    table_ref,
    table_t_ref,
    sems,
):
    rows, feat = table_ref.shape
    block = user_t_ref.shape[1]
    chunks = rows // chunk
    step = pl.program_id(0)
    last = pl.num_programs(0) - 1

    def at(c):
        return pl.ds(pl.multiple_of(c * chunk, chunk), chunk)

    def fetches(c):
        return (
            pltpu.make_async_copy(table_hbm.at[at(c)], table_ref.at[at(c)], sems.at[0, c]),
            pltpu.make_async_copy(mask_hbm.at[at(c)], mask_ref.at[at(c)], sems.at[1, c]),
        )

    turned = pltpu.make_async_copy(table_t_hbm, table_t_ref, sems.at[2, 0])

    @pl.when(step == 0)
    def _():
        for c in range(chunks):
            for fetch in fetches(c):
                fetch.start()
        turned.start()

    label = label_ref[...]
    user_t = user_t_ref[...]
    user = user_t.astype(F32).T.astype(BF)
    sublane = lax.broadcasted_iota(jnp.int32, (8, block), 0)

    def hits(c):
        place = label - c * chunk - sublane
        return jnp.concatenate([place == 8 * g for g in range(chunk // 8)], axis=0)


    def fold(v, op):
        return op(v.reshape(chunk // 8, 8, block), axis=0)

    def first(c, carry):
        @pl.when(step == 0)
        def _():
            for fetch in fetches(c):
                fetch.wait()

        peak, pos = carry
        s = jnp.dot(table_ref[at(c), :], user_t, preferred_element_type=F32)
        pos = pos + fold(jnp.where(hits(c), s, 0.0), jnp.sum)
        s = s + jnp.concatenate([mask_ref[at(c), :].astype(F32)] * (block // LANES), axis=1)
        logits[at(c), :] = s
        return jnp.maximum(peak, fold(s, jnp.max)), pos

    peak, pos = lax.fori_loop(
        0,
        chunks,
        first,
        (jnp.full((8, block), -jnp.inf, F32), jnp.zeros((8, block), F32)),
    )
    pos = jnp.sum(pos, axis=0, keepdims=True)
    peak = jnp.maximum(jnp.max(peak, axis=0, keepdims=True), pos)

    def second(c, total):
        p = jnp.exp(logits[at(c), :] - peak)
        logits[at(c), :] = p
        return total + fold(p, jnp.sum)

    total = lax.fori_loop(0, chunks, second, jnp.zeros((8, block), F32))
    pos_exp = jnp.exp(pos - peak)
    total = jnp.sum(total, axis=0, keepdims=True) + pos_exp
    loss_ref[...] = peak + jnp.log(total) - pos
    scale = inv_count / total
    d_pos = (pos_exp / total - 1.0) * inv_count

    @pl.when(step == 0)
    def _():
        turned.wait()

    def back(add, store):
        def third(c, d_user_t):
            d = logits[at(c), :] * scale
            d = jnp.where(hits(c), d + d_pos, d).astype(BF)
            term = jnp.dot(d, user, preferred_element_type=F32)
            if add:
                term = grad_sum[at(c), :] + term
            if store:
                grad_ref[at(c), :] = term.astype(BF)
            else:
                grad_sum[at(c), :] = term
            return d_user_t + jnp.dot(table_t_ref[:, at(c)], d, preferred_element_type=F32)

        d_user_t = lax.fori_loop(0, chunks, third, jnp.zeros((feat, block), F32))
        d_user_ref[...] = d_user_t.T.astype(BF)

    @pl.when(step == 0)
    def _():
        back(False, False)

    @pl.when((step > 0) & (step < last))
    def _():
        back(True, False)

    @pl.when(step == last)
    def _():
        back(True, True)


def softmax_call(mask, table, table_t, user, labels, block=512, chunk=4096):
    n, feat = user.shape
    rows = table.shape[0]
    across = lambda h: pl.BlockSpec((h, block), lambda i: (0, i))
    any_place = pl.BlockSpec(memory_space=pl.ANY)
    return pl.pallas_call(
        functools.partial(softmax_body, 1.0 / n, chunk),
        grid=(n // block,),
        in_specs=[any_place] * 3
        + [across(feat), across(1)],
        out_specs=[pl.BlockSpec((block, feat), lambda i: (i, 0)), whole_vmem(), across(1)],
        out_shape=[
            jax.ShapeDtypeStruct((n, feat), BF),
            jax.ShapeDtypeStruct((rows, feat), BF),
            jax.ShapeDtypeStruct((1, n), F32),
        ],
        scratch_shapes=[
            pltpu.VMEM((rows, block), F32),
            pltpu.VMEM((rows, feat), F32),
            pltpu.VMEM((rows, LANES), BF),
            pltpu.VMEM((rows, feat), BF),
            pltpu.VMEM((feat, rows), BF),
            pltpu.SemaphoreType.DMA((3, rows // chunk)),
        ],
        compiler_params=params(46),
        name="sampled_softmax",
    )(mask, table, table_t, user.T, labels.reshape(1, n))


def sampled_mask(negatives, rows):
    high = lax.broadcasted_iota(jnp.int32, (rows // LANES, negatives.shape[0]), 0)
    low = lax.broadcasted_iota(jnp.int32, (LANES, negatives.shape[0]), 0)
    high_hot = (high == negatives[None, :] // LANES).astype(BF)
    low_hot = (low == negatives[None, :] % LANES).astype(BF)
    sampled = right_product(high_hot, low_hot).reshape(rows, 1)
    return jnp.broadcast_to(jnp.where(sampled > 0.5, 0.0, -1e30).astype(BF), (rows, LANES))


def left_product(first_op, second_op):
    return lax.dot_general(
        first_op, second_op, (((0,), (0,)), ((), ())), preferred_element_type=F32
    )


def right_product(first_op, second_op):
    return lax.dot_general(
        first_op, second_op, (((1,), (1,)), ((), ())), preferred_element_type=F32
    )


def gelu_back(pre_value, d_act):
    unused, pull = jax.vjp(jax.nn.gelu, pre_value)
    return pull(d_act)[0]


def in_range_ids(ids, lengths, offset):
    slot = lax.broadcasted_iota(jnp.int32, ids.shape, 1)
    kept = jnp.where(slot < lengths[:, None], ids + offset, -1)
    return jnp.pad(kept, ((0, 0), (0, LANES // 2 - ids.shape[1])), constant_values=-1)


def local(
    hot_table,
    tail_table,
    word_table,
    out_table,
    w_first,
    b_first,
    w_second,
    b_second,
    w_third,
    b_third,
    dense_feats,
    hist_ids,
    hist_len,
    search_ids,
    search_len,
    requests,
    labels,
    negatives,
):
    feat = hot_table.shape[1]
    hot_rows = hot_table.shape[0]
    owners, per_owner = requests.shape
    slots = owners * per_owner
    examples_dev = hist_ids.shape[0]
    examples_all = examples_dev * lax.axis_size("group") * lax.axis_size("wide")
    shard_rows = tail_table.shape[0]
    hist_float = hist_len[:, None].astype(F32)
    search_float = search_len[:, None].astype(F32)

    asked = lax.all_to_all(requests, "wide", split_axis=0, concat_axis=0, tiled=True)
    looked = gather_call(asked, tail_table)
    returned = lax.all_to_all(
        looked.reshape(owners, per_owner, feat), "wide", split_axis=0, concat_axis=0, tiled=True
    ).reshape(slots, feat)

    asked, negatives, looked = lax.optimization_barrier((asked, negatives, looked))
    ids = jnp.concatenate(
        [
            in_range_ids(hist_ids, hist_len, 0),
            in_range_ids(search_ids, search_len, hot_rows + slots),
        ],
        axis=1,
    )
    out_table_t = out_table.T
    mask = sampled_mask(negatives, out_table.shape[0])
    unroll = 16
    cuts = (16, 16, 16, 32, 16, 16, 16)
    edges = [sum(cuts[:i]) for i in range(len(cuts) + 1)]
    asked_parts = [asked[:, i:j].reshape(-1) for i, j in zip(edges, edges[1:])]
    plan = row_plan(jnp.concatenate(asked_parts), shard_rows, unroll)
    ids, out_table_t, mask, plan, looked = lax.optimization_barrier(
        (ids, out_table_t, mask, plan, looked)
    )
    hot_counts, slot_counts, word_counts, hot_sum, word_sum = counts_call(
        ids, hot_table, word_table, slots
    )

    hist_mean = (hot_sum + jnp.dot(slot_counts.astype(BF), returned, preferred_element_type=F32)) / hist_float
    search_mean = word_sum / search_float
    hist_mean, search_mean = hist_mean.astype(BF), search_mean.astype(BF)
    dense = jnp.pad(dense_feats, ((0, 0), (0, -w_first.shape[0] % LANES)))
    inputs = jnp.concatenate([hist_mean, search_mean, dense_feats], axis=1)
    pre_first = jnp.dot(inputs, w_first, preferred_element_type=F32) + b_first.astype(F32)
    act_first = jax.nn.gelu(pre_first).astype(BF)
    pre_second = jnp.dot(act_first, w_second, preferred_element_type=F32) + b_second.astype(F32)
    act_second = jax.nn.gelu(pre_second).astype(BF)
    user = (jnp.dot(act_second, w_third, preferred_element_type=F32) + b_third.astype(F32)).astype(
        BF
    )

    d_user, out_grad, per_example = softmax_call(mask, out_table, out_table_t, user, labels)
    d_pre_second = gelu_back(pre_second, right_product(d_user, w_third)).astype(BF)
    d_pre_first = gelu_back(pre_first, right_product(d_pre_second, w_second)).astype(BF)
    d_inputs = right_product(d_pre_first, w_first[: 2 * feat])

    packed = gradients_call(
        d_inputs,
        (hist_float, search_float),
        (hist_mean, search_mean, dense),
        act_first,
        act_second,
        d_pre_first,
        d_pre_second,
        d_user,
        per_example,
        jnp.sum(d_pre_first.astype(F32), axis=0)[None],
        jnp.sum(d_pre_second.astype(F32), axis=0)[None],
        (hot_counts, word_counts),
    )
    packed = (*packed, out_grad)
    w3_rows = w_third.shape[0]
    packed, slot_counts = lax.optimization_barrier((packed, slot_counts))
    summed = lax.psum(packed, ("group", "wide"))

    slot_grads = slot_spread_call(slot_counts, hist_float, d_inputs, feat, cuts, 4)
    owed = []
    for part in slot_grads:
        if owed:
            part, owed[-1] = lax.optimization_barrier((part, owed[-1]))
        owed.append(lax.all_to_all(part, "wide", split_axis=0, concat_axis=0, tiled=True))
    owed = [x.reshape(-1, feat) for x in owed]
    own = add_rows_call(plan, owed, shard_rows, unroll, 4)
    others = [lax.ppermute(x, "group", [(0, 1), (1, 0)]) for x in own]
    tail_grad = add_pair_call(own, others)
    summed, tail_grad = lax.optimization_barrier((summed, tail_grad))
    hot_all, word_all, out_all, w2_all, w1_all, w3_all, loss_value, b1_all, b2_all, b3_all = widen_call(
        (summed[0], summed[1], summed[5], summed[3]),
        summed[2],
        summed[4],
        w_first.shape[0],
        w3_rows,
        examples_dev // feat,
        (b_first.shape[0], b_second.shape[0], b_third.shape[0]),
        examples_all,
        2,
    )
    return (
        loss_value[0, 0],
        hot_all,
        tail_grad,
        word_all,
        out_all,
        w1_all,
        b1_all[0],
        w2_all,
        b2_all[0],
        w3_all,
        b3_all[0],
    )


def solution(mesh):
    split = ("group", "wide")
    in_specs = (
        (P(), P("wide", None))
        + (P(),) * 8
        + (P(split, None), P(split, None), P(split), P(split, None), P(split), P(split, None))
        + (P(split), P())
    )
    out_specs = (P(), P(), P("wide", None)) + (P(),) * 8
    return jax.shard_map(local, mesh=mesh, in_specs=in_specs, out_specs=out_specs, check_vma=False)
```
